256 devices in a mesh: ctx: 8 (over y_lo, x), head: 32 (over z, y_hi, core).
Axes of the slice: x: 4, y: 4 (y_hi: 2, y_lo: 2; y = y_hi * 2 + y_lo), z: 8, core: 2. Of those that a mesh axis runs over, the one named last changes fastest.
Arguments:
- layer_input: bfloat16 [4096, 4096], P('ctx', 'head'), may hold values from -6 to 6
- grad_core: bfloat16 [4096, 4096], P('ctx', 'head'), may hold values from -6 to 6
- w_in: bfloat16 [4096, 32, 4, 128], P(None, 'head'), may hold values from -0.09375 to 0.09375
- beta_proj: bfloat16 [32, 4096], P('head'), may hold values from -0.046875 to 0.046875
- beta_bias: float32 [32], P('head'), may hold values from -6 to 6
Outputs:
- grad_input: bfloat16 [4096, 4096], P('ctx', 'head')
- grad_w_in: bfloat16 [4096, 32, 4, 128], P('ctx', 'head')
- grad_beta_proj: float32 [32, 4096], P('head', 'ctx')
The draws below stay inside these ranges and needn't reach their ends.
All inputs are finite; a program needn't handle non-finite values.
Results may differ from the reference program's by a relative error of at most 0.024.
Values may be sent and summed in bfloat16 or wider, within the bound.
No kernel may reach another device: no remote copies, remote signals or barrier semaphores. Data moves between devices by JAX's collectives and lax.ppermute only.
A program may use at most 128 MiB of HBM per device.

```python
import jax
import jax.numpy as jnp
from jax import lax

D = 4096
HD = 128
SUB = 64
TOK_DEV = 512
HEADS = 32
SEQ = 4096
N_CTX = 8


def draw_beta_bias(key, part):
    key = jax.random.fold_in(key, 7)
    sign_key, size_key = jax.random.split(key)
    signs = jnp.where(jax.random.bernoulli(sign_key, 0.5, (HEADS,)), 1.0, -1.0)
    sizes = jax.random.uniform(size_key, (HEADS,), minval=0.0, maxval=6.0)
    return (signs * sizes).astype(jnp.float32)


def steps_of(key, extent, pieces, smallest, top_value):
    loudness, own = 1.0, jax.random.fold_in(key, 6)
    for dim, parts in pieces:
        steps = jnp.exp(jax.random.uniform(jax.random.fold_in(own, dim), (parts,), jnp.float32, smallest / len(pieces), top_value / len(pieces)))
        loudness = loudness * jnp.repeat(steps, extent[dim] // parts).reshape([-1 if axis == dim else 1 for axis in range(len(extent))])
    return loudness


def scatter_about(own_key, dims, spread, most, pieces=(), kind=jnp.bfloat16):
    gain = steps_of(own_key, dims, pieces, -0.22, 0.18) if pieces else 1.0
    drawn = jax.random.normal(own_key, dims, jnp.float32) * spread * gain
    return jnp.minimum(jnp.maximum(drawn, -most), most).astype(kind)


def setup_inputs(seed: int = 0) -> dict:
    seeds = jax.random.split(jax.random.key(seed), 6)
    layer_input = scatter_about(seeds[0], (SEQ, D), 1.0, 6.0, ((0, 8), (1, 32)))
    grad_core = scatter_about(seeds[1], (SEQ, HEADS * HD), 1.0, 6.0, ((0, 8), (1, 32)))
    w_in = scatter_about(seeds[2], (D, HEADS, 4, HD), D ** -0.5, 0.09375, ((1, 32),))
    beta_proj = scatter_about(seeds[3], (HEADS, D), (4 * D) ** -0.5, 0.046875, ((0, 32),))
    beta_bias = draw_beta_bias(jax.random.fold_in(seeds[5], 71), 0)
    return {"layer_input": layer_input, "grad_core": grad_core, "w_in": w_in, "beta_proj": beta_proj, "beta_bias": beta_bias}


TEMP = 8.0
EPS = 1e-06
HIGH = lax.Precision.HIGHEST

def highest(left_side, right_side):
    return jnp.matmul(left_side, right_side, precision=HIGH)

def unit_rows(matrix):
    return matrix / jnp.sqrt(lax.optimization_barrier(jnp.sum(matrix * matrix, axis=-1, keepdims=True)) + EPS)

def reflect_block(queries, keys_in, reflect, beta_values):
    block_size = reflect.shape[0]
    head_width = reflect.shape[1]
    lower_strict = jnp.tril(jnp.ones((block_size, block_size), dtype=bool), -1)
    lower_incl = jnp.tril(jnp.ones((block_size, block_size), dtype=bool))
    gram_matrix = highest(reflect, reflect.T)
    system = jnp.eye(block_size, dtype=jnp.float32) + jnp.where(lower_strict, beta_values[:, None] * gram_matrix, 0.0)
    factor = jax.scipy.linalg.solve_triangular(system, jnp.diag(beta_values), lower=True, unit_diagonal=True)
    query_on = jnp.where(lower_incl, highest(queries, reflect.T), 0.0)
    key_on = jnp.where(lower_strict.T, highest(keys_in, reflect.T), 0.0)
    query_mix = highest(query_on, factor)
    query_hat = queries - highest(query_mix, reflect)
    key_hat = keys_in - highest(highest(key_on, factor.T), reflect)
    transform = jnp.eye(head_width, dtype=jnp.float32) - highest(reflect.T, highest(factor, reflect))
    diagonal = TEMP * (highest(queries, keys_in.T) - highest(query_mix, key_on.T))
    return (query_hat, key_hat, transform, diagonal)

def prepare(projected, logits):
    head_width = projected.shape[1] // 4
    length = projected.shape[0]
    block_count = length // SUB
    queries = unit_rows(projected[:, :head_width])
    keys_in = unit_rows(projected[:, head_width:2 * head_width])
    values = projected[:, 2 * head_width:3 * head_width].astype(jnp.bfloat16)
    reflect = unit_rows(projected[:, 3 * head_width:])
    beta_values = 2.0 * jax.nn.sigmoid(logits)
    block_shape = (block_count, SUB, head_width)
    query_hat, key_hat, transforms, diagonals = jax.vmap(reflect_block)(queries.reshape(block_shape), keys_in.reshape(block_shape), reflect.reshape(block_shape), beta_values.reshape(block_count, SUB))
    block_index = jnp.arange(block_count, dtype=jnp.int32)

    def forward_step(carried, inputs):
        prefix, moved_keys = carried
        query_block, key_block, transform, diagonal, position = inputs
        query_dev = highest(query_block, prefix)
        cross_scores = TEMP * jnp.einsum('id,njd->inj', query_block, moved_keys, precision=HIGH)
        is_here = block_index == position
        cross_scores = jnp.where(is_here[None, :, None], diagonal[:, None, :], cross_scores)
        moved_keys = jnp.einsum('njd,ed->nje', moved_keys, transform, precision=HIGH)
        moved_keys = jnp.where(is_here[:, None, None], key_block[None], moved_keys)
        return ((highest(transform, prefix), moved_keys), (query_dev, cross_scores.reshape(SUB, length)))
    initial = (jnp.eye(head_width, dtype=jnp.float32), jnp.zeros(block_shape, jnp.float32))
    (device_map, unused), (query_dev, scores) = lax.scan(forward_step, initial, (query_hat, key_hat, transforms, diagonals, block_index))

    def backward_step(suffix, inputs):
        key_block, transform = inputs
        return (highest(suffix, transform), highest(key_block, suffix.T))
    unused_map, key_dev = lax.scan(backward_step, jnp.eye(head_width, dtype=jnp.float32), (key_hat, transforms), reverse=True)
    return (query_dev.reshape(length, head_width).astype(jnp.bfloat16), key_dev.reshape(length, head_width).astype(jnp.bfloat16), values, device_map, scores.reshape(length, length))

def head_grads(layer_input, weights, beta_row, bias, grad_head):
    shard_count = N_CTX
    length = TOK_DEV
    weights_flat = weights.reshape(D, 4 * HD)
    projected = jnp.dot(layer_input.astype(jnp.float32), weights_flat.astype(jnp.float32), preferred_element_type=jnp.float32)
    logits = jnp.dot(layer_input.astype(jnp.float32), beta_row.astype(jnp.float32), preferred_element_type=jnp.float32) + bias
    row_index = jnp.arange(length)
    causal = row_index[:, None] >= row_index[None, :]
    outputs, pullbacks, core_parts, input_parts = ([], [], [], [])
    for shard in range(shard_count):
        lower_row = shard * length
        result, pullback = jax.vjp(prepare, projected[lower_row:lower_row + length], logits[lower_row:lower_row + length])
        outputs.append(result)
        pullbacks.append(pullback)
        core_parts.append(grad_head[lower_row:lower_row + length])
        input_parts.append(layer_input[lower_row:lower_row + length])
    moved_keys = {}
    for source in range(shard_count):
        current = outputs[source][1]
        for target in range(source + 1, shard_count):
            moved_keys[target, source] = current
            current = highest(current.astype(jnp.float32), outputs[target][3].T).astype(jnp.bfloat16)
    log_totals, row_deltas = ([], [])
    for target in range(shard_count):
        query_dev, key_dev, values, device_map, scores_in = outputs[target]
        exp_in = jnp.where(causal, jnp.exp(scores_in), 0.0)
        total = lax.optimization_barrier(jnp.sum(exp_in, axis=1))
        accumulated = jnp.dot(exp_in.astype(jnp.bfloat16).astype(jnp.float32), values.astype(jnp.float32), preferred_element_type=jnp.float32)
        for source in range(target):
            scores = TEMP * jnp.einsum('id,jd->ij', query_dev.astype(jnp.float32), moved_keys[target, source].astype(jnp.float32), preferred_element_type=jnp.float32)
            exp_scores = jnp.exp(scores)
            total = total + lax.optimization_barrier(jnp.sum(exp_scores, axis=1))
            accumulated = accumulated + jnp.dot(exp_scores.astype(jnp.bfloat16).astype(jnp.float32), outputs[source][2].astype(jnp.float32), preferred_element_type=jnp.float32)
        attended = accumulated / total[:, None]
        log_totals.append(jnp.log(total))
        row_deltas.append(lax.optimization_barrier(jnp.sum(core_parts[target].astype(jnp.float32) * attended, axis=1)))
    grad_query = [jnp.zeros((length, HD), jnp.float32) for shard in range(shard_count)]
    grad_values = [jnp.zeros((length, HD), jnp.float32) for shard in range(shard_count)]
    grad_scores_in = []
    through = {}
    for target in range(shard_count):
        query_dev, key_dev, values, device_map, scores_in = outputs[target]
        grad_rows = core_parts[target]
        log_total = log_totals[target]
        row_delta = row_deltas[target]
        prob_in = jnp.where(causal, jnp.exp(scores_in - log_total[:, None]), 0.0)
        grad_prob = jnp.einsum('id,jd->ij', grad_rows.astype(jnp.float32), values.astype(jnp.float32), preferred_element_type=jnp.float32)
        grad_scores_in.append(prob_in * (grad_prob - row_delta[:, None]))
        grad_values[target] = grad_values[target] + jnp.einsum('ij,id->jd', prob_in.astype(jnp.bfloat16).astype(jnp.float32), grad_rows.astype(jnp.float32), preferred_element_type=jnp.float32)
        for source in range(target):
            key_block = moved_keys[target, source]
            value_block = outputs[source][2]
            scores = TEMP * jnp.einsum('id,jd->ij', query_dev.astype(jnp.float32), key_block.astype(jnp.float32), preferred_element_type=jnp.float32)
            prob_block = jnp.exp(scores - log_total[:, None])
            grad_prob = jnp.einsum('id,jd->ij', grad_rows.astype(jnp.float32), value_block.astype(jnp.float32), preferred_element_type=jnp.float32)
            grad_score = (prob_block * (grad_prob - row_delta[:, None])).astype(jnp.bfloat16)
            grad_query[target] = grad_query[target] + TEMP * jnp.dot(grad_score.astype(jnp.float32), key_block.astype(jnp.float32), preferred_element_type=jnp.float32)
            through[target, source] = TEMP * jnp.einsum('ij,id->jd', grad_score.astype(jnp.float32), query_dev.astype(jnp.float32), preferred_element_type=jnp.float32)
            grad_values[source] = grad_values[source] + jnp.einsum('ij,id->jd', prob_block.astype(jnp.bfloat16).astype(jnp.float32), grad_rows.astype(jnp.float32), preferred_element_type=jnp.float32)
    grad_maps = [jnp.zeros((HD, HD), jnp.float32) for shard in range(shard_count)]
    grad_keys = []
    for source in range(shard_count):
        carried = jnp.zeros((length, HD), jnp.float32)
        for target in range(shard_count - 1, source, -1):
            grad_maps[target] = grad_maps[target] + jnp.einsum('jd,je->de', carried, moved_keys[target, source].astype(jnp.float32), precision=HIGH)
            carried = highest(carried, outputs[target][3]) + through[target, source]
        grad_keys.append(carried)
    proj_parts, logit_parts = ([], [])
    weight_total = jnp.zeros((D, 4 * HD), jnp.float32)
    beta_total = jnp.zeros((D,), jnp.float32)
    for shard in range(shard_count):
        cotangents = (grad_query[shard].astype(jnp.bfloat16), grad_keys[shard].astype(jnp.bfloat16), grad_values[shard].astype(jnp.bfloat16), grad_maps[shard], grad_scores_in[shard])
        grad_proj, grad_logit = pullbacks[shard](cotangents)
        grad_proj = grad_proj.astype(jnp.bfloat16)
        grad_logit = grad_logit.astype(jnp.bfloat16)
        proj_parts.append(grad_proj)
        logit_parts.append(grad_logit)
        partial_w = jnp.dot(input_parts[shard].T.astype(jnp.float32), grad_proj.astype(jnp.float32), preferred_element_type=jnp.float32).astype(jnp.bfloat16)
        partial_b = jnp.dot(input_parts[shard].T.astype(jnp.float32), grad_logit.astype(jnp.float32), preferred_element_type=jnp.float32).astype(jnp.bfloat16)
        partial_w, partial_b = lax.optimization_barrier((partial_w, partial_b))
        weight_total = weight_total + partial_w.astype(jnp.float32)
        beta_total = beta_total + partial_b.astype(jnp.float32)
    all_proj = jnp.concatenate(proj_parts, axis=0)
    all_logit = jnp.concatenate(logit_parts, axis=0)
    input_grad = jnp.dot(all_proj.astype(jnp.float32), weights_flat.T.astype(jnp.float32), preferred_element_type=jnp.float32)
    input_grad = input_grad + all_logit.astype(jnp.float32)[:, None] * beta_row.astype(jnp.float32)[None, :]
    return (input_grad, weight_total, beta_total)

def reference(layer_input, grad_core, w_in, beta_proj, beta_bias):
    weight_heads = jnp.moveaxis(w_in, 1, 0)
    core_heads = jnp.moveaxis(grad_core.reshape(SEQ, HEADS, HD), 1, 0)

    def one_head(total_grad, inputs):
        weights, beta_row, bias, grad_head = inputs
        input_grad, weight_grad, beta_grad = head_grads(layer_input, weights, beta_row, bias, grad_head)
        return (total_grad + input_grad, (weight_grad, beta_grad))
    total_grad, (weight_grads, beta_grads) = lax.scan(one_head, jnp.zeros((SEQ, D), jnp.float32), (weight_heads, beta_proj, beta_bias, core_heads))
    grad_w_in = jnp.moveaxis(weight_grads.reshape(HEADS, D, 4, HD), 0, 1).astype(jnp.bfloat16)
    return (total_grad.astype(jnp.bfloat16), grad_w_in, beta_grads)
```

```python
import jax
import jax.numpy as jnp
from jax import lax
from jax.experimental import pallas as pl
from jax.experimental.pallas import tpu as pltpu
from jax.sharding import Mesh
from jax.sharding import PartitionSpec as P

HD = 128
LEN = 512
HALF = 256
SHARDS = 8
CTX = ("y_lo", "x")
HEAD = ("z", "y_hi", "core")
DEPTH = 8
WIDE = 4
OFFSETS = (0, -1, 1, -2, 2, -3, 3, -4)
TALL = LEN + 16
TEMP = 8.0
EPS = 1e-06
F32 = jnp.float32
BF16 = jnp.bfloat16
NN = ((1,), (0,))
NT = ((1,), (1,))
TN = ((0,), (0,))


def mxu(left, right, dims):
    return lax.dot_general(left, right, (dims, ((), ())), preferred_element_type=F32)


def one(left, right, dims=NN):
    return mxu(left.astype(BF16), right.astype(BF16), dims)


def split(matrix):
    high = matrix.astype(BF16)
    return high, (matrix - high.astype(F32)).astype(BF16)


def three(left, right, dims=NN):
    left_high, left_low = left
    right_high, right_low = right
    return (
        mxu(left_high, right_high, dims)
        + mxu(left_high, right_low, dims)
        + mxu(left_low, right_high, dims)
    )


def rows_of(size):
    return lax.broadcasted_iota(jnp.int32, (size, size), 0)


def cols_of(size):
    return lax.broadcasted_iota(jnp.int32, (size, size), 1)


def part(matrix, rows, cols):
    if isinstance(matrix, tuple):
        return tuple(half[rows, cols] for half in matrix)
    return matrix[rows, cols]


TOP = slice(0, HALF)
BOT = slice(HALF, LEN)
ALL = slice(0, LEN)


def lower_times_lower(left, right, product):
    top = product(part(left, TOP, TOP), part(right, TOP, TOP), NN)
    corner = product(part(left, BOT, ALL), part(right, ALL, TOP), NN)
    bottom = product(part(left, BOT, BOT), part(right, BOT, BOT), NN)
    zero = jnp.zeros((HALF, HALF), F32)
    return jnp.concatenate(
        [jnp.concatenate([top, zero], 1), jnp.concatenate([corner, bottom], 1)], 0
    )


def lower_times_upper_t(left, right, product):
    top = product(part(left, TOP, TOP), part(right, TOP, TOP), NT)
    corner = product(part(left, BOT, TOP), part(right, TOP, TOP), NT)
    bottom = product(part(left, BOT, ALL), part(right, BOT, ALL), NT)
    zero = jnp.zeros((HALF, HALF), F32)
    return jnp.concatenate(
        [jnp.concatenate([top, zero], 1), jnp.concatenate([corner, bottom], 1)], 0
    )


def upper_times_lower(left, right, product):
    top = product(part(left, TOP, ALL), part(right, ALL, TOP), NN)
    corner = product(part(left, BOT, BOT), part(right, BOT, TOP), NN)
    bottom = product(part(left, BOT, BOT), part(right, BOT, BOT), NN)
    zero = jnp.zeros((HALF, HALF), F32)
    return jnp.concatenate(
        [jnp.concatenate([top, zero], 1), jnp.concatenate([corner, bottom], 1)], 0
    )


def upper_times_upper(left, right, product, dims):
    if dims == NN:
        top = product(part(left, TOP, TOP), part(right, TOP, TOP), NN)
        corner = product(part(left, TOP, ALL), part(right, ALL, BOT), NN)
        bottom = product(part(left, BOT, BOT), part(right, BOT, BOT), NN)
    else:
        top = product(part(left, TOP, TOP), part(right, TOP, TOP), NT)
        corner = product(part(left, TOP, ALL), part(right, BOT, ALL), NT)
        bottom = product(part(left, BOT, BOT), part(right, BOT, BOT), NT)
    zero = jnp.zeros((HALF, HALF), F32)
    return jnp.concatenate(
        [jnp.concatenate([top, corner], 1), jnp.concatenate([zero, bottom], 1)], 0
    )


def unit_scale(matrix):
    return 1.0 / jnp.sqrt(jnp.sum(matrix * matrix, axis=1, keepdims=True) + EPS)


def inverse_blocks(blocks):
    size = HD
    row, col = rows_of(size), cols_of(size)
    found = []
    for block in blocks:
        first = ((row >> 1) == (col >> 1)) & (row > col)
        found.append(jnp.where(row == col, 1.0, 0.0) - jnp.where(first, block, 0.0))
    step = 1
    while (2 << step) <= size:
        pair = ((row >> (step + 1)) == (col >> (step + 1))) & ((row >> step) > (col >> step))
        halves = [split(inverse) for inverse in found]
        mixed = [
            split(three(split(jnp.where(pair, block, 0.0)), half))
            for block, half in zip(blocks, halves)
        ]
        found = [
            inverse - three(half, mix) for inverse, half, mix in zip(found, halves, mixed)
        ]
        step += 1
    return found


def first_kernel(proj_ref, lcol_ref, lrow_ref, pack_ref, inv_ref, unit_ref, y_ref, vt_ref):
    proj = proj_ref[...]
    keys_raw = proj[:, HD : 2 * HD]
    reflect_raw = proj[:, 3 * HD :]
    queries_raw = proj[:, :HD]
    queries = queries_raw * unit_scale(queries_raw)
    keys = keys_raw * unit_scale(keys_raw)
    reflect = reflect_raw * unit_scale(reflect_raw)
    unit_ref[:, :HD] = queries
    unit_ref[:, HD : 2 * HD] = keys
    unit_ref[:, 2 * HD :] = reflect
    beta_col = 2.0 * jax.nn.sigmoid(lcol_ref[...])
    beta_row = 2.0 * jax.nn.sigmoid(lrow_ref[...])
    reflect_s = split(reflect)
    row, col = rows_of(HD), cols_of(HD)

    def system(i, j):
        rows, cols = slice(i * HD, (i + 1) * HD), slice(j * HD, (j + 1) * HD)
        gram = three(part(reflect_s, rows, slice(None)), part(reflect_s, cols, slice(None)), NT)
        gram = beta_col[rows] * gram
        return jnp.where(row > col, gram, 0.0) if i == j else gram

    solved = inverse_blocks([system(i, i) for i in range(4)])
    solved_s = [split(inverse) for inverse in solved]
    pairs = []
    for i in (0, 2):
        mix = three(split(system(i + 1, i)), solved_s[i])
        corner = -three(solved_s[i + 1], split(mix))
        zero = jnp.zeros((HD, HD), F32)
        pairs.append(
            jnp.concatenate(
                [
                    jnp.concatenate([solved[i], zero], 1),
                    jnp.concatenate([corner, solved[i + 1]], 1),
                ],
                0,
            )
        )
    top_s, bottom_s = split(pairs[0]), split(pairs[1])
    wide = three(part(reflect_s, BOT, slice(None)), part(reflect_s, TOP, slice(None)), NT)
    mix = three(split(beta_col[BOT] * wide), top_s)
    corner = -three(bottom_s, split(mix))
    inv_ref[TOP, TOP] = pairs[0]
    inv_ref[TOP, BOT] = jnp.zeros((HALF, HALF), F32)
    inv_ref[BOT, TOP] = corner
    inv_ref[BOT, BOT] = pairs[1]
    corner_s = split(corner)
    scaled_s = split(beta_col * reflect)
    y_top = three(top_s, part(scaled_s, TOP, slice(None)))
    y_bottom = three(corner_s, part(scaled_s, TOP, slice(None))) + three(
        bottom_s, part(scaled_s, BOT, slice(None))
    )
    y_all = jnp.concatenate([y_top, y_bottom], 0)
    y_ref[...] = y_all
    vt_top = three(part(reflect_s, TOP, slice(None)), top_s, TN) + three(
        part(reflect_s, BOT, slice(None)), corner_s, TN
    )
    vt_bottom = three(part(reflect_s, BOT, slice(None)), bottom_s, TN)
    vt_all = jnp.concatenate([vt_top, vt_bottom], 1) * beta_row
    vt_ref[...] = vt_all
    big_row, big_col = rows_of(LEN), cols_of(LEN)
    key_on = jnp.where(big_col > big_row, three(split(keys), reflect_s, NT), 0.0)
    pack_ref[:LEN] = (keys - three(split(key_on), split(vt_all), NT)).astype(BF16)
    change = jnp.where(row == col, 1.0, 0.0) - three(reflect_s, split(y_all), TN)
    change_high, change_low = split(change)
    pack_ref[LEN : LEN + HD] = change_high
    pack_ref[LEN + HD :] = change_low


def second_kernel(
    unit_ref, inv_ref, lrow_ref, y_ref, v_ref,
    qd_ref, ut_ref, exp_ref, query_on_ref, query_low_ref, key_on_ref, key_low_ref, total_ref, acc_ref,
):
    queries = split(unit_ref[:, :HD])
    keys = split(unit_ref[:, HD : 2 * HD])
    reflect = split(unit_ref[:, 2 * HD :])
    beta_row = 2.0 * jax.nn.sigmoid(lrow_ref[...])
    row, col = rows_of(LEN), cols_of(LEN)
    query_on = jnp.where(row >= col, three(queries, reflect, NT), 0.0)
    qd_ref[...] = (
        TEMP * (unit_ref[:, :HD] - three(split(query_on), split(y_ref[...])))
    ).astype(BF16)
    query_on_t = jnp.where(row <= col, three(reflect, queries, NT), 0.0)
    query_on_t = split(query_on_t)
    query_on_ref[...] = query_on_t[0]
    query_low_ref[...] = query_on_t[1]
    key_on = jnp.where(row < col, three(keys, reflect, NT), 0.0)
    key_on_t = split(jnp.where(row > col, three(reflect, keys, NT), 0.0))
    key_on_ref[...] = key_on_t[0]
    key_low_ref[...] = key_on_t[1]
    factor = split(inv_ref[...] * beta_row)
    key_on = split(key_on)
    ut = split(upper_times_upper(key_on, factor, three, NT))
    ut_ref[...] = ut[0]
    scores = TEMP * (three(keys, queries, NT) - upper_times_upper(ut, query_on_t, three, NN))
    exped = jnp.where(row <= col, jnp.exp(scores), 0.0)
    total_ref[...] = jnp.sum(exped, axis=0, keepdims=True)
    exped = exped.astype(BF16)
    exp_ref[...] = exped
    acc_ref[...] = mxu(v_ref[...], exped, TN)


def third_kernel(
    where_ref, qd_ref, own_v, left_v, right_v, far_v0, far_v1, own_k, left_k, right_k, far_k0, far_k1,
    core_ref, total_ref, acc_ref,
    out_ref, grad_q_ref, core_scaled_ref, delta_ref, exp_ref, values_ref, keys_ref,
):
    my_y, my_x = where_ref[0], where_ref[1]
    me = my_y * WIDE + my_x

    def place(shift, other):
        line = my_y if other == 0 else 1 - my_y
        return line * WIDE + lax.rem(my_x + shift + WIDE, WIDE)

    for shift, value_part, key_part in (
        (0, own_v, own_k), (-1, left_v, left_k), (1, right_v, right_k),
    ):
        for other in range(2):
            spot = place(shift, other)
            values_ref[spot] = value_part[other]
            keys_ref[spot] = key_part[other]
    values_ref[place(2, 0)] = far_v0[...]
    keys_ref[place(2, 0)] = far_k0[...]
    values_ref[place(2, 1)] = far_v1[...]
    keys_ref[place(2, 1)] = far_k1[...]
    queries = qd_ref[...]
    total = total_ref[...]
    acc = acc_ref[...]
    eye = jnp.where(rows_of(HD) == cols_of(HD), 1.0, 0.0)
    carry = [None] * (SHARDS - 1)
    moved = [None] * (SHARDS - 1)

    def change_of(b):
        return keys_ref[b, LEN : LEN + HD], keys_ref[b, LEN + HD :]

    for b in range(SHARDS - 2, -1, -1):
        if b == SHARDS - 2:
            carry[b] = eye
        else:
            follow = three(split(carry[b + 1]), change_of(b + 1))
            carry[b] = jnp.where(b >= me - 1, eye, follow)
        carry_s = split(carry[b])
        keys = keys_ref[b, :LEN]
        moved[b] = (mxu(keys, carry_s[0], NT) + mxu(keys, carry_s[1], NT)).astype(BF16)
        bias = jnp.where(b < me, 0.0, -1e30).astype(F32)
        exped = jnp.exp(mxu(moved[b], queries, NT) + bias)
        total = total + jnp.sum(exped, axis=0, keepdims=True)
        exped = exped.astype(BF16)
        exp_ref[b] = exped
        acc = acc + mxu(values_ref[b], exped, TN)
    inverse_total = 1.0 / total
    core_t = core_ref[...].astype(F32).T
    delta = jnp.sum(core_t * acc, axis=0, keepdims=True) * inverse_total * inverse_total
    delta_ref[...] = delta
    core_t = core_t * inverse_total
    core_scaled = core_t.T.astype(BF16)
    core_scaled_ref[...] = core_scaled
    grad_q = jnp.zeros((HD, LEN), F32)
    inner = jnp.zeros((HD, HD), F32)
    out_ref[SHARDS - 1] = jnp.zeros(out_ref.shape[1:], BF16)
    for b in range(SHARDS - 1):
        keys = keys_ref[b, :LEN]
        exped = exp_ref[b]
        change = mxu(values_ref[b], core_scaled, NT)
        grad_scores = (exped.astype(F32) * (change - delta)).astype(BF16)
        grad_q = grad_q + mxu(moved[b], grad_scores, TN)
        through = mxu(grad_scores, queries, NN).astype(BF16)
        carry_s = split(carry[b])
        out_ref[b, :LEN, :HD] = (
            mxu(through, carry_s[0], NN) + mxu(through, carry_s[1], NN)
        ).astype(BF16)
        out_ref[b, :LEN, HD:] = mxu(exped, core_scaled, NN).astype(BF16)
        if b >= 1:
            live = jnp.where(b < me, 1.0, 0.0).astype(F32)
            out_map = (one(carry[b], inner, TN) * live).astype(BF16)
        else:
            out_map = jnp.zeros((HD, HD), BF16)
        out_ref[b, LEN:, :HD] = out_map[: HD // 2]
        out_ref[b, LEN:, HD:] = out_map[HD // 2 :]
        if b < SHARDS - 2:
            step = mxu(through, keys, TN)
            inner = step if b == 0 else three(split(inner), change_of(b), NT) + step
    grad_q_ref[...] = TEMP * grad_q


def fourth_kernel(
    unit_ref, inv_ref, lrow_ref, y_ref, v_ref, ut_ref, exp_ref, query_on_ref, query_low_ref,
    key_on_ref, key_low_ref, core_scaled_ref, delta_ref, grad_q_ref,
    dq_ref, dk_ref, dw_ref, gv_ref, aq_ref, nk_ref, xtn_ref, inv_t_ref, inv_low_ref,
):
    queries = unit_ref[:, :HD].astype(BF16)
    keys = unit_ref[:, HD : 2 * HD].astype(BF16)
    reflect = unit_ref[:, 2 * HD :].astype(BF16)
    row, col = rows_of(LEN), cols_of(LEN)
    core_scaled = core_scaled_ref[...]
    exped = exp_ref[...]
    gv_ref[...] = mxu(exped, core_scaled, NN)
    change = mxu(v_ref[...], core_scaled, NT)
    grad_scores = (TEMP * exped.astype(F32) * (change - delta_ref[...])).astype(BF16)
    grad_q_t = grad_q_ref[...].astype(BF16)
    grad_q = grad_q_t.astype(F32).T.astype(BF16)
    query_on_t = query_on_ref[...]
    key_on_t = (key_on_ref[...], key_low_ref[...])
    inner = mxu(query_on_t, grad_scores, NT) + mxu(query_low_ref[...], grad_scores, NT)
    inner = split(jnp.where(row > col, inner, 0.0))
    aq_ref[...] = mxu(query_on_t, grad_q, NN) + mxu(query_low_ref[...], grad_q, NN)
    nk_ref[...] = lower_times_upper_t(inner, key_on_t, three)
    inverse_t = split(inv_ref[...].T)
    inv_t_ref[...] = inverse_t[0]
    inv_low_ref[...] = inverse_t[1]
    xtn_ref[...] = upper_times_lower(inverse_t[0], inner[0], mxu)
    d_query_on = mxu(ut_ref[...], grad_scores, TN) + one(y_ref[...], grad_q, NT)
    d_query_on = -jnp.where(row <= col, d_query_on, 0.0)
    d_query_on = d_query_on.astype(BF16)
    dq_t = grad_q_t.astype(F32) + mxu(keys, grad_scores, TN) + mxu(reflect, d_query_on, TN)
    dq_ref[...] = dq_t.T
    dw_ref[...] = mxu(d_query_on, queries, NN)
    dk_ref[...] = mxu(grad_scores, queries, NN)


def unit_back(grad, unit, raw):
    return (grad - unit * jnp.sum(unit * grad, axis=1, keepdims=True)) * unit_scale(raw)


def fifth_kernel(
    proj_ref, unit_ref, inv_ref, inv_t_ref, inv_low_ref, lcol_ref, lrow_ref, vt_ref, key_on_ref, key_low_ref,
    dq_ref, dk_ref, dw_ref, gv_ref, aq_ref, nk_ref, xtn_ref, back_ref,
    grad_ref,
):
    received = back_ref[0].astype(F32)
    for a in range(1, SHARDS):
        received = received + back_ref[a].astype(F32)
    d_keys = received[:LEN, :HD].astype(BF16)
    d_map = split(jnp.concatenate([received[LEN:, :HD], received[LEN:, HD:]], 0))
    grad_ref[:LEN, 2 * HD : 3 * HD] = (gv_ref[...] + received[:LEN, HD:]).astype(BF16)
    queries = unit_ref[:, :HD]
    keys = unit_ref[:, HD : 2 * HD]
    reflect = unit_ref[:, 2 * HD :]
    reflect_s = split(reflect)
    beta_col = 2.0 * jax.nn.sigmoid(lcol_ref[...])
    beta_row = 2.0 * jax.nn.sigmoid(lrow_ref[...])
    row, col = rows_of(LEN), cols_of(LEN)
    factor = split(inv_ref[...] * beta_row)
    on_keys = mxu(key_on_ref[...], d_keys, NN) + mxu(key_low_ref[...], d_keys, NN)
    side_q = split(aq_ref[...] + three(reflect_s, d_map, NN))
    side_k = split(on_keys + three(reflect_s, d_map, NT))
    dw = dw_ref[...] - three(factor, side_k, NN)
    dw_t = -three(side_q, factor, TN)
    d_factor = nk_ref[...] + three(side_q, reflect_s, NT) + three(reflect_s, split(on_keys), NT)
    d_factor = -jnp.where(row >= col, d_factor, 0.0)
    mid = upper_times_lower((inv_t_ref[...], inv_low_ref[...]), split(d_factor), three)
    mid = jnp.where(row >= col, mid, 0.0)
    d_system = lower_times_upper_t(split(mid), factor, three)
    d_system = -jnp.where(row > col, d_system, 0.0)
    gram = three(reflect_s, reflect_s, NT)
    d_beta = split(jnp.where(row == col, mid, 0.0) + d_system * gram)
    ones = jnp.ones((TALL - LEN, LEN), BF16)
    d_beta = mxu(ones, d_beta[0], NT) + mxu(ones, d_beta[1], NT)
    d_logit = d_beta * beta_row * (1.0 - 0.5 * beta_row)
    first = lax.broadcasted_iota(jnp.int32, (TALL - LEN, LEN), 0) == 0
    grad_ref[LEN:] = jnp.where(first, d_logit, 0.0).astype(BF16)
    d_gram = split(beta_col * d_system)
    dw = dw + three(d_gram, reflect_s, NN)
    dw_t = dw_t + three(reflect_s, d_gram, TN)
    d_key_on = beta_col * xtn_ref[...] + one(vt_ref[...], d_keys.T, TN)
    d_key_on = -jnp.where(row > col, d_key_on, 0.0)
    d_key_on = d_key_on.astype(BF16)
    dk_t = mxu(reflect_s[0], d_key_on, TN)
    dw = dw + one(d_key_on, keys, NN) + dw_t.T
    dk = d_keys.astype(F32) + dk_ref[...] + dk_t.T
    proj = proj_ref[...]
    grad_ref[:LEN, :HD] = unit_back(dq_ref[...], queries, proj[:, :HD]).astype(BF16)
    grad_ref[:LEN, HD : 2 * HD] = unit_back(dk, keys, proj[:, HD : 2 * HD]).astype(BF16)
    grad_ref[:LEN, 3 * HD :] = unit_back(dw, reflect, proj[:, 3 * HD :]).astype(BF16)


def shape(*dims, dtype=F32):
    return jax.ShapeDtypeStruct(dims, dtype)


def call(kernel, outs, *args, scalars=0, scratch=(), flops=2 * 10**9):
    vmem = pl.BlockSpec(memory_space=pltpu.VMEM)
    smem = pl.BlockSpec(memory_space=pltpu.SMEM)
    return pl.pallas_call(
        kernel,
        out_shape=outs,
        in_specs=[smem] * scalars + [vmem] * (len(args) - scalars),
        out_specs=jax.tree.map(lambda out: vmem, outs),
        scratch_shapes=list(scratch),
        compiler_params=pltpu.CompilerParams(vmem_limit_bytes=16 * 2**20),
        cost_estimate=pl.CostEstimate(flops=flops, bytes_accessed=4 * 2**20, transcendentals=0),
    )(*args)


def project_kernel(
    where_ref, bias_ref, near_ref, near_swap, far_ref, far_swap, weight_ref, beta_ref,
    all_ref, proj_ref, lcol_ref, lrow_ref, value_ref,
):
    my_z, my_y, my_core = where_ref[2], where_ref[3], where_ref[4]
    for slot, offset in enumerate(OFFSETS):
        z = lax.rem(my_z + offset + DEPTH, DEPTH)
        own, other = (near_ref, near_swap) if slot < 5 else (far_ref, far_swap)
        place = slot if slot < 5 else slot - 5
        for side in range(2):
            y = my_y if side == 0 else 1 - my_y
            base = z * 4 + y * 2
            all_ref[base + my_core] = own[place, side]
            all_ref[base + 1 - my_core] = other[place, side]
    proj = jnp.zeros((LEN, 4 * HD), F32)
    col = jnp.zeros((LEN, 8), F32)
    row = jnp.zeros((8, LEN), F32)
    for j in range(DEPTH):
        features = jnp.concatenate([all_ref[4 * j + k] for k in range(4)], axis=1)
        proj = proj + mxu(features, weight_ref[j * LEN : (j + 1) * LEN], NN)
        beta = jnp.broadcast_to(beta_ref[j : j + 1, :], (8, LEN)).astype(BF16)
        col = col + mxu(features, beta, NT)
        row = row + mxu(beta, features, NT)
    proj_ref[...] = proj
    lcol_ref[...] = col[:, :1] + bias_ref[0]
    lrow_ref[...] = row[:1] + bias_ref[0]
    value_ref[...] = proj[:, 2 * HD : 3 * HD].astype(BF16)


def weight_kernel(all_ref, grad_ref, out_ref):
    grad = grad_ref[:LEN]
    logit = grad_ref[LEN:]
    for e in range(SHARDS):
        features = jnp.concatenate([all_ref[4 * e + k] for k in range(4)], axis=1)
        out_ref[e, :LEN] = mxu(features, grad, TN).astype(BF16)
        out_ref[e, LEN:] = mxu(logit, features, NN).astype(BF16)


def feature_kernel(
    where_ref, own_ref, other_ref, weight_ref, other_weight, own_beta, other_beta, out_ref
):
    my_z, my_y, my_core = where_ref[2], where_ref[3], where_ref[4]
    extra = TALL - LEN
    own, other = own_ref[:LEN], other_ref[:LEN]
    logits = jnp.concatenate([own_ref[LEN:], other_ref[LEN:]], axis=0)
    for slot, offset in enumerate(OFFSETS):
        z = lax.rem(my_z + offset + DEPTH, DEPTH)
        betas = jnp.concatenate(
            [
                jnp.broadcast_to(own_beta[z], (extra, HALF)),
                jnp.broadcast_to(other_beta[z], (extra, HALF)),
            ],
            axis=0,
        ).astype(BF16)
        base = pl.multiple_of(z * LEN + my_core * HD, HD)
        own_weight = jnp.concatenate(
            [weight_ref[pl.ds(base, HD)], weight_ref[pl.ds(base + HALF, HD)]], axis=0
        )
        term = mxu(own, own_weight, NT) + mxu(other, other_weight[z], NT)
        term = (term + mxu(logits, betas, TN)).astype(BF16)
        out_ref[slot, my_y] = term[:, :HD]
        out_ref[slot, 1 - my_y] = term[:, HD:]


def swapped(value, axis):
    return lax.ppermute(value, axis, [(0, 1), (1, 0)])


def turned(value, axis, step):
    count = lax.axis_size(axis)
    return lax.ppermute(value, axis, [(i, (i + step) % count) for i in range(count)])


def plus(*terms):
    total = terms[0].astype(F32)
    for term in terms[1:]:
        total = total + term.astype(F32)
    return total


def gather_features(block, w_in, core):
    pair = jnp.stack([block, swapped(block, "y_hi")])
    up, down = turned(pair, "z", 1), turned(pair, "z", -1)
    weights = w_in.reshape(w_in.shape[0], 4 * HD)
    up, down, weights = lax.optimization_barrier((up, down, weights))
    up_two, down_two = turned(up, "z", 1), turned(down, "z", -1)
    by_core = weights.reshape(2 * DEPTH, 2, HD, 4 * HD)
    away = lax.dynamic_index_in_dim(by_core, 1 - core, 1, False).reshape(DEPTH, HALF, 4 * HD)
    up_two, down_two, away = lax.optimization_barrier((up_two, down_two, away))
    near = jnp.stack([pair, up, down, up_two, down_two])
    near_swap = swapped(near, "core")
    up_three, down_three = turned(up_two, "z", 1), turned(down_two, "z", -1)
    last = jnp.stack([turned(up_three[0], "z", 1), turned(down_three[1], "z", -1)])
    far = jnp.stack([up_three, down_three, last])
    return near, near_swap, far, swapped(far, "core"), weights, away


def gather_shards(block):
    pair = jnp.stack([block, swapped(block, "y_lo")])
    left, right = turned(pair, "x", 1), turned(pair, "x", -1)
    return pair, left, right, turned(left[0], "x", 1), turned(right[1], "x", -1)


def scatter_heads(terms):
    def at(offset):
        return terms[OFFSETS.index(offset)]

    up = turned(at(-4)[0], "z", 1)
    down = turned(at(-4)[1], "z", -1)
    up = jnp.stack([plus(at(3)[0], up).astype(BF16), at(3)[1]])
    down = jnp.stack([at(-3)[0], plus(at(-3)[1], down).astype(BF16)])
    for step in (2, 1):
        up = plus(turned(up, "z", 1), at(step)).astype(BF16)
        down = plus(turned(down, "z", -1), at(-step)).astype(BF16)
    total = plus(turned(up, "z", 1), turned(down, "z", -1), at(0))
    return total[0] + swapped(total[1].astype(BF16), "y_hi").astype(F32)


def on_device(layer_input, grad_core, w_in, beta_proj, beta_bias):
    where = jnp.stack([lax.axis_index(axis) for axis in CTX + HEAD]).astype(jnp.int32)
    core = lax.axis_index("core")
    near, near_swap, far, far_swap, weights_flat, away = gather_features(layer_input, w_in, core)
    other_weight = swapped(away, "core")
    beta_by_core = beta_proj[0].reshape(2 * DEPTH, 2, HD)
    own_beta = lax.dynamic_index_in_dim(beta_by_core, core, 1, False).reshape(DEPTH, 1, HALF)
    other_beta = swapped(
        lax.dynamic_index_in_dim(beta_by_core, 1 - core, 1, False).reshape(DEPTH, 1, HALF), "core"
    )
    everything, projected, logit_col, logit_row, values = call(
        project_kernel,
        [
            shape(4 * DEPTH, LEN, HD, dtype=BF16),
            shape(LEN, 4 * HD),
            shape(LEN, 1),
            shape(1, LEN),
            shape(LEN, HD, dtype=BF16),
        ],
        where,
        beta_bias,
        near,
        near_swap,
        far,
        far_swap,
        weights_flat,
        beta_proj[0].reshape(DEPTH, LEN).astype(F32),
        scalars=2,
    )
    value_parts = gather_shards(values)
    sent, inverse, unit, y_side, vt_side = call(
        first_kernel,
        [
            shape(LEN + 2 * HD, HD, dtype=BF16),
            shape(LEN, LEN),
            shape(LEN, 3 * HD),
            shape(LEN, HD),
            shape(HD, LEN),
        ],
        projected,
        logit_col,
        logit_row,
    )
    key_parts = gather_shards(sent)
    query_dev, ut_side, exp_in, query_on, query_low, key_on, key_low, total_in, acc_in = call(
        second_kernel,
        [
            shape(LEN, HD, dtype=BF16),
            shape(LEN, LEN, dtype=BF16),
            shape(LEN, LEN, dtype=BF16),
            shape(LEN, LEN, dtype=BF16),
            shape(LEN, LEN, dtype=BF16),
            shape(LEN, LEN, dtype=BF16),
            shape(LEN, LEN, dtype=BF16),
            shape(1, LEN),
            shape(HD, LEN),
        ],
        unit,
        inverse,
        logit_row,
        y_side,
        values,
    )
    back, grad_query, core_scaled, delta = call(
        third_kernel,
        [
            shape(SHARDS, LEN + HD // 2, 2 * HD, dtype=BF16),
            shape(HD, LEN),
            shape(LEN, HD, dtype=BF16),
            shape(1, LEN),
        ],
        where,
        query_dev,
        *value_parts,
        *key_parts,
        grad_core,
        total_in,
        acc_in,
        scalars=1,
        scratch=[
            pltpu.VMEM((SHARDS - 1, LEN, LEN), BF16),
            pltpu.VMEM((SHARDS, LEN, HD), BF16),
            pltpu.VMEM((SHARDS, LEN + 2 * HD, HD), BF16),
        ],
    )
    returned = lax.all_to_all(back, CTX, 0, 0)
    dq, dk, dw, gv, aq, nk, xtn, inverse_t, inverse_low = call(
        fourth_kernel,
        [
            shape(LEN, HD),
            shape(LEN, HD),
            shape(LEN, HD),
            shape(LEN, HD),
            shape(LEN, HD),
            shape(LEN, LEN),
            shape(LEN, LEN),
            shape(LEN, LEN, dtype=BF16),
            shape(LEN, LEN, dtype=BF16),
        ],
        unit,
        inverse,
        logit_row,
        y_side,
        values,
        ut_side,
        exp_in,
        query_on,
        query_low,
        key_on,
        key_low,
        core_scaled,
        delta,
        grad_query,
    )
    grad_proj = call(
        fifth_kernel,
        shape(TALL, 4 * HD, dtype=BF16),
        projected,
        unit,
        inverse,
        inverse_t,
        inverse_low,
        logit_col,
        logit_row,
        vt_side,
        key_on,
        key_low,
        dq,
        dk,
        dw,
        gv,
        aq,
        nk,
        xtn,
        returned,
    )
    other_proj = swapped(grad_proj, "core")
    weight_terms = call(
        weight_kernel,
        shape(SHARDS, TALL, 4 * HD, dtype=BF16),
        everything,
        grad_proj,
    )
    feature_terms = call(
        feature_kernel,
        shape(DEPTH, 2, LEN, HD, dtype=BF16),
        where,
        grad_proj,
        other_proj,
        weights_flat,
        other_weight,
        own_beta.astype(F32),
        other_beta.astype(F32),
        scalars=1,
    )
    summed = jnp.sum(lax.all_to_all(weight_terms, CTX, 0, 0).astype(F32), axis=0)
    grad_input = scatter_heads(feature_terms).astype(BF16)
    grad_w_in = summed[:LEN].astype(BF16).reshape(LEN, 1, 4, HD)
    return (grad_input, grad_w_in, summed[LEN : LEN + 1])


def solution(mesh):
    parts = Mesh(mesh.devices.reshape(2, WIDE, DEPTH, 2, 2), CTX + HEAD)
    in_specs = (P(CTX, HEAD), P(CTX, HEAD), P(None, HEAD, None, None), P(HEAD, None), P(HEAD))
    out_specs = (P(CTX, HEAD), P(CTX, HEAD, None, None), P(HEAD, CTX))
    return jax.shard_map(
        on_device, mesh=parts, in_specs=in_specs, out_specs=out_specs, check_vma=False
    )
```

```python
import jax
import jax.numpy as jnp
from jax import lax
from jax.experimental import pallas as pl
from jax.experimental.pallas import tpu as pltpu
from jax.sharding import Mesh
from jax.sharding import PartitionSpec as P

HD = 128
LEN = 512
HALF = 256
SHARDS = 8
CTX = ("y_lo", "x")
HEAD = ("z", "y_hi", "core")
DEPTH = 8
WIDE = 4
OFFSETS = (0, -1, 1, -2, 2, -3, 3, -4)
TALL = LEN + 16
NEAR = OFFSETS[:5]
FAR = OFFSETS[5:]
PACK = LEN + 2 * HD + LEN
CUT = LEN + HD
TEMP = 8.0
EPS = 1e-06
F32 = jnp.float32
BF16 = jnp.bfloat16
NN = ((1,), (0,))
NT = ((1,), (1,))
TN = ((0,), (0,))


def mxu(left, right, dims):
    return lax.dot_general(left, right, (dims, ((), ())), preferred_element_type=F32)


def one(left, right, dims=NN):
    return mxu(left.astype(BF16), right.astype(BF16), dims)


def split(matrix):
    high = matrix.astype(BF16)
    return high, (matrix - high.astype(F32)).astype(BF16)


def three(left, right, dims=NN):
    left_high, left_low = left
    right_high, right_low = right
    return (
        mxu(left_high, right_high, dims)
        + mxu(left_high, right_low, dims)
        + mxu(left_low, right_high, dims)
    )


def rows_of(size):
    return lax.broadcasted_iota(jnp.int32, (size, size), 0)


def cols_of(size):
    return lax.broadcasted_iota(jnp.int32, (size, size), 1)


def part(matrix, rows, cols):
    if isinstance(matrix, tuple):
        return tuple(half[rows, cols] for half in matrix)
    return matrix[rows, cols]


TOP = slice(0, HALF)
BOT = slice(HALF, LEN)
ALL = slice(0, LEN)


def lower_times_lower(left, right, product):
    top = product(part(left, TOP, TOP), part(right, TOP, TOP), NN)
    corner = product(part(left, BOT, ALL), part(right, ALL, TOP), NN)
    bottom = product(part(left, BOT, BOT), part(right, BOT, BOT), NN)
    zero = jnp.zeros((HALF, HALF), F32)
    return jnp.concatenate(
        [jnp.concatenate([top, zero], 1), jnp.concatenate([corner, bottom], 1)], 0
    )


def lower_times_upper_t(left, right, product):
    top = product(part(left, TOP, TOP), part(right, TOP, TOP), NT)
    corner = product(part(left, BOT, TOP), part(right, TOP, TOP), NT)
    bottom = product(part(left, BOT, ALL), part(right, BOT, ALL), NT)
    zero = jnp.zeros((HALF, HALF), F32)
    return jnp.concatenate(
        [jnp.concatenate([top, zero], 1), jnp.concatenate([corner, bottom], 1)], 0
    )


def upper_times_lower(left, right, product):
    top = product(part(left, TOP, ALL), part(right, ALL, TOP), NN)
    corner = product(part(left, BOT, BOT), part(right, BOT, TOP), NN)
    bottom = product(part(left, BOT, BOT), part(right, BOT, BOT), NN)
    zero = jnp.zeros((HALF, HALF), F32)
    return jnp.concatenate(
        [jnp.concatenate([top, zero], 1), jnp.concatenate([corner, bottom], 1)], 0
    )


def upper_times_upper(left, right, product, dims):
    if dims == NN:
        top = product(part(left, TOP, TOP), part(right, TOP, TOP), NN)
        corner = product(part(left, TOP, ALL), part(right, ALL, BOT), NN)
        bottom = product(part(left, BOT, BOT), part(right, BOT, BOT), NN)
    else:
        top = product(part(left, TOP, TOP), part(right, TOP, TOP), NT)
        corner = product(part(left, TOP, ALL), part(right, BOT, ALL), NT)
        bottom = product(part(left, BOT, BOT), part(right, BOT, BOT), NT)
    zero = jnp.zeros((HALF, HALF), F32)
    return jnp.concatenate(
        [jnp.concatenate([top, corner], 1), jnp.concatenate([zero, bottom], 1)], 0
    )


def unit_scale(matrix):
    return 1.0 / jnp.sqrt(jnp.sum(matrix * matrix, axis=1, keepdims=True) + EPS)


def inverse_blocks(blocks):
    size = HD
    row, col = rows_of(size), cols_of(size)
    found = []
    for block in blocks:
        first = ((row >> 1) == (col >> 1)) & (row > col)
        found.append(jnp.where(row == col, 1.0, 0.0) - jnp.where(first, block, 0.0))
    step = 1
    while (2 << step) <= size:
        pair = ((row >> (step + 1)) == (col >> (step + 1))) & ((row >> step) > (col >> step))
        halves = [split(inverse) for inverse in found]
        mixed = [
            split(three(split(jnp.where(pair, block, 0.0)), half))
            for block, half in zip(blocks, halves)
        ]
        found = [
            inverse - three(half, mix) for inverse, half, mix in zip(found, halves, mixed)
        ]
        step += 1
    return found


def first_kernel(
    proj_ref, lcol_ref, lrow_ref, pack_ref, inv_ref, unit_ref, y_ref, vt_ref,
):
    proj = proj_ref[...]
    keys_raw = proj[:, HD : 2 * HD]
    reflect_raw = proj[:, 3 * HD :]
    queries_raw = proj[:, :HD]
    queries = queries_raw * unit_scale(queries_raw)
    keys = keys_raw * unit_scale(keys_raw)
    reflect = reflect_raw * unit_scale(reflect_raw)
    unit_ref[...] = jnp.concatenate([queries, keys, reflect], axis=1)
    beta_col = 2.0 * jax.nn.sigmoid(lcol_ref[...])
    beta_row = 2.0 * jax.nn.sigmoid(lrow_ref[...])
    reflect_s = split(reflect)
    row, col = rows_of(HD), cols_of(HD)

    def system(i, j):
        rows, cols = slice(i * HD, (i + 1) * HD), slice(j * HD, (j + 1) * HD)
        gram = three(part(reflect_s, rows, slice(None)), part(reflect_s, cols, slice(None)), NT)
        gram = beta_col[rows] * gram
        return jnp.where(row > col, gram, 0.0) if i == j else gram

    solved = inverse_blocks([system(i, i) for i in range(4)])
    solved_s = [split(inverse) for inverse in solved]
    pairs = []
    for i in (0, 2):
        mix = three(split(system(i + 1, i)), solved_s[i])
        corner = -three(solved_s[i + 1], split(mix))
        zero = jnp.zeros((HD, HD), F32)
        pairs.append(
            jnp.concatenate(
                [
                    jnp.concatenate([solved[i], zero], 1),
                    jnp.concatenate([corner, solved[i + 1]], 1),
                ],
                0,
            )
        )
    top_s, bottom_s = split(pairs[0]), split(pairs[1])
    wide = three(part(reflect_s, BOT, slice(None)), part(reflect_s, TOP, slice(None)), NT)
    mix = three(split(beta_col[BOT] * wide), top_s)
    corner = -three(bottom_s, split(mix))
    zero = jnp.zeros((HALF, HALF), F32)
    inv_ref[...] = jnp.concatenate(
        [jnp.concatenate([pairs[0], zero], 1), jnp.concatenate([corner, pairs[1]], 1)], 0
    )
    corner_s = split(corner)
    scaled_s = split(beta_col * reflect)
    y_top = three(top_s, part(scaled_s, TOP, slice(None)))
    y_bottom = three(corner_s, part(scaled_s, TOP, slice(None))) + three(
        bottom_s, part(scaled_s, BOT, slice(None))
    )
    y_all = jnp.concatenate([y_top, y_bottom], 0)
    y_ref[...] = y_all
    vt_top = three(part(reflect_s, TOP, slice(None)), top_s, TN) + three(
        part(reflect_s, BOT, slice(None)), corner_s, TN
    )
    vt_bottom = three(part(reflect_s, BOT, slice(None)), bottom_s, TN)
    vt_all = jnp.concatenate([vt_top, vt_bottom], 1) * beta_row
    vt_ref[...] = vt_all
    big_row, big_col = rows_of(LEN), cols_of(LEN)
    key_on = jnp.where(big_col > big_row, three(split(keys), reflect_s, NT), 0.0)
    pack_ref[:LEN] = (keys - three(split(key_on), split(vt_all), NT)).astype(BF16)
    change = jnp.where(row == col, 1.0, 0.0) - three(reflect_s, split(y_all), TN)
    change_high, change_low = split(change)
    pack_ref[LEN : LEN + HD] = change_high
    pack_ref[LEN + HD : LEN + 2 * HD] = change_low
    pack_ref[LEN + 2 * HD :] = proj[:, 2 * HD : 3 * HD].astype(BF16)


def second_kernel(
    unit_ref, inv_ref, lrow_ref, y_ref, v_ref,
    qd_ref, ut_ref, exp_ref, query_on_ref, query_low_ref, key_on_ref, key_low_ref, total_ref, acc_ref,
):
    queries = split(unit_ref[:, :HD])
    keys = split(unit_ref[:, HD : 2 * HD])
    reflect = split(unit_ref[:, 2 * HD :])
    beta_row = 2.0 * jax.nn.sigmoid(lrow_ref[...])
    row, col = rows_of(LEN), cols_of(LEN)
    query_on = jnp.where(row >= col, three(queries, reflect, NT), 0.0)
    qd_ref[...] = (
        TEMP * (unit_ref[:, :HD] - three(split(query_on), split(y_ref[...])))
    ).astype(BF16)
    query_on_t = jnp.where(row <= col, three(reflect, queries, NT), 0.0)
    query_on_t = split(query_on_t)
    query_on_ref[...] = query_on_t[0]
    query_low_ref[...] = query_on_t[1]
    key_on = jnp.where(row < col, three(keys, reflect, NT), 0.0)
    key_on_t = split(jnp.where(row > col, three(reflect, keys, NT), 0.0))
    key_on_ref[...] = key_on_t[0]
    key_low_ref[...] = key_on_t[1]
    factor = split(inv_ref[...] * beta_row)
    key_on = split(key_on)
    ut = split(upper_times_upper(key_on, factor, three, NT))
    ut_ref[...] = ut[0]
    scores = TEMP * (three(keys, queries, NT) - upper_times_upper(ut, query_on_t, three, NN))
    exped = jnp.where(row <= col, jnp.exp(scores), 0.0)
    total_ref[...] = jnp.sum(exped, axis=0, keepdims=True)
    exped = exped.astype(BF16)
    exp_ref[...] = exped
    acc_ref[...] = mxu(v_ref[LEN + 2 * HD :], exped, TN)


def third_kernel(
    flow, where_ref, qd_ref, own, own_left, own_right, own_far0, own_far1,
    other, other_left, other_right, other_far0, other_far1,
    core_ref, total_ref, acc_ref,
    out_hbm, grad_q_hbm, core_scaled_hbm, delta_hbm,
    exp_ref, keys_ref, out_ref, grad_q_ref, core_scaled_ref, delta_ref,
):
    my_y, my_x = where_ref[0], where_ref[1]
    me = my_y * WIDE + my_x
    for line, parts in (
        (my_y, (own, own_left, own_right, own_far0, own_far1)),
        (1 - my_y, (other, other_left, other_right, other_far0, other_far1)),
    ):
        for shift, part_ref in ((0, parts[0]), (-1, parts[1]), (1, parts[2])):
            keys_ref[line * WIDE + lax.rem(my_x + shift + WIDE, WIDE)] = part_ref[...]
        far = line * WIDE + lax.rem(my_x + 2, WIDE)
        keys_ref[far, :CUT] = parts[3][...]
        keys_ref[far, CUT:] = parts[4][...]
    queries = qd_ref[...]
    total = total_ref[...]
    acc = acc_ref[...]
    eye = jnp.where(rows_of(HD) == cols_of(HD), 1.0, 0.0)
    carry = [None] * (SHARDS - 1)
    moved = [None] * (SHARDS - 1)

    def change_of(b):
        return keys_ref[b, LEN : LEN + HD], keys_ref[b, LEN + HD : LEN + 2 * HD]

    for b in range(SHARDS - 2, -1, -1):
        if b == SHARDS - 2:
            carry[b] = eye
        else:
            follow = three(split(carry[b + 1]), change_of(b + 1))
            carry[b] = jnp.where(b >= me - 1, eye, follow)
        carry_s = split(carry[b])
        keys = keys_ref[b, :LEN]
        moved[b] = (mxu(keys, carry_s[0], NT) + mxu(keys, carry_s[1], NT)).astype(BF16)
        bias = jnp.where(b < me, 0.0, -1e30).astype(F32)
        exped = jnp.exp(mxu(moved[b], queries, NT) + bias)
        total = total + jnp.sum(exped, axis=0, keepdims=True)
        exped = exped.astype(BF16)
        exp_ref[b] = exped
        acc = acc + mxu(keys_ref[b, LEN + 2 * HD :], exped, TN)
    inverse_total = 1.0 / total
    core_t = core_ref[...].astype(F32).T
    delta = jnp.sum(core_t * acc, axis=0, keepdims=True) * inverse_total * inverse_total
    delta_ref[...] = delta
    core_t = core_t * inverse_total
    core_scaled = core_t.T.astype(BF16)
    core_scaled_ref[...] = core_scaled
    grad_q = jnp.zeros((HD, LEN), F32)
    inner = jnp.zeros((HD, HD), F32)
    out_ref[SHARDS - 1] = jnp.zeros(out_ref.shape[1:], BF16)
    flow.send(out_ref.at[SHARDS - 1], out_hbm.at[SHARDS - 1])
    flow.send(core_scaled_ref, core_scaled_hbm)
    flow.send(delta_ref, delta_hbm)
    for b in range(SHARDS - 1):
        keys = keys_ref[b, :LEN]
        exped = exp_ref[b]
        change = mxu(keys_ref[b, LEN + 2 * HD :], core_scaled, NT)
        grad_scores = (exped.astype(F32) * (change - delta)).astype(BF16)
        grad_q = grad_q + mxu(moved[b], grad_scores, TN)
        through = mxu(grad_scores, queries, NN).astype(BF16)
        carry_s = split(carry[b])
        out_ref[b, :LEN, :HD] = (
            mxu(through, carry_s[0], NN) + mxu(through, carry_s[1], NN)
        ).astype(BF16)
        out_ref[b, :LEN, HD:] = mxu(exped, core_scaled, NN).astype(BF16)
        if b >= 1:
            live = jnp.where(b < me, 1.0, 0.0).astype(F32)
            out_map = (one(carry[b], inner, TN) * live).astype(BF16)
        else:
            out_map = jnp.zeros((HD, HD), BF16)
        out_ref[b, LEN:, :HD] = out_map[: HD // 2]
        out_ref[b, LEN:, HD:] = out_map[HD // 2 :]
        flow.send(out_ref.at[b], out_hbm.at[b])
        if b < SHARDS - 2:
            step = mxu(through, keys, TN)
            inner = step if b == 0 else three(split(inner), change_of(b), NT) + step
    grad_q_ref[...] = TEMP * grad_q
    flow.send(grad_q_ref, grad_q_hbm)
    flow.finish()


def fourth_kernel(
    proj_ref, unit_ref, inv_ref, lrow_ref, y_ref, ut_ref, exp_ref, query_on_ref, query_low_ref,
    key_on_ref, key_low_ref, core_scaled_ref, delta_ref, grad_q_ref,
    dq_ref, dk_ref, dw_ref, gv_ref, taq_ref, vb_ref, low_ref, xtn_ref, fac_ref, fac_low_ref, scale_ref,
):
    queries = unit_ref[:, :HD].astype(BF16)
    keys = unit_ref[:, HD : 2 * HD].astype(BF16)
    reflect_s = split(unit_ref[:, 2 * HD :])
    reflect = reflect_s[0]
    beta_row = 2.0 * jax.nn.sigmoid(lrow_ref[...])
    row, col = rows_of(LEN), cols_of(LEN)
    core_scaled = core_scaled_ref[...]
    exped = exp_ref[...]
    gv_ref[...] = mxu(exped, core_scaled, NN)
    change = one(proj_ref[:, 2 * HD : 3 * HD], core_scaled, NT)
    grad_scores = (TEMP * exped.astype(F32) * (change - delta_ref[...])).astype(BF16)
    grad_q_t = grad_q_ref[...].astype(BF16)
    grad_q = grad_q_t.astype(F32).T.astype(BF16)
    query_on_t = query_on_ref[...]
    key_on_t = (key_on_ref[...], key_low_ref[...])
    inner = mxu(query_on_t, grad_scores, NT) + mxu(query_low_ref[...], grad_scores, NT)
    inner = split(jnp.where(row > col, inner, 0.0))
    side_q = mxu(query_on_t, grad_q, NN) + mxu(query_low_ref[...], grad_q, NN)
    inverse = inv_ref[...]
    factor = split(inverse * beta_row)
    fac_ref[...] = factor[0]
    fac_low_ref[...] = factor[1]
    inverse_t = split(inverse.T)
    taq_ref[...] = three(inverse_t, split(side_q))
    vb_ref[...] = three(inverse_t, reflect_s)
    mid = lower_times_upper_t(inner, key_on_t, three)
    mid = upper_times_lower(inverse_t, split(mid), three)
    low_ref[...] = lower_times_upper_t(split(mid), factor, three)
    diagonal = jnp.sum(jnp.where(row == col, mid, 0.0), axis=1, keepdims=True)
    xtn_ref[...] = upper_times_lower(inverse_t[0], inner[0], mxu).astype(BF16)
    d_query_on = mxu(ut_ref[...], grad_scores, TN) + one(y_ref[...], grad_q, NT)
    d_query_on = -jnp.where(row <= col, d_query_on, 0.0)
    d_query_on = d_query_on.astype(BF16)
    dq_t = grad_q_t.astype(F32) + mxu(keys, grad_scores, TN) + mxu(reflect, d_query_on, TN)
    scales = [unit_scale(proj_ref[:, k * HD : (k + 1) * HD]) for k in (0, 1, 3)]
    dq_ref[...] = unit_back(dq_t.T, unit_ref[:, :HD], scales[0]).astype(BF16)
    lane = lax.broadcasted_iota(jnp.int32, (LEN, HD), 1)
    scale_ref[...] = jnp.where(
        lane < HD // 4, scales[1], jnp.where(lane < HD // 2, scales[2], diagonal)
    )
    dw_ref[...] = mxu(d_query_on, queries, NN)
    dk_ref[...] = mxu(grad_scores, queries, NN)


def unit_back(grad, unit, scale):
    return (grad - unit * jnp.sum(unit * grad, axis=1, keepdims=True)) * scale


def fifth_kernel(
    unit_ref, fac_ref, fac_low_ref, lcol_ref, lrow_ref, y_ref, vt_ref, key_on_ref, key_low_ref,
    dq_ref, dk_ref, dw_ref, gv_ref, taq_ref, vb_ref, low_ref, xtn_ref, scale_ref, back_ref,
    grad_ref,
):
    received = back_ref[0].astype(F32)
    for a in range(1, SHARDS):
        received = received + back_ref[a].astype(F32)
    d_keys = received[:LEN, :HD].astype(BF16)
    d_map = split(jnp.concatenate([received[LEN:, :HD], received[LEN:, HD:]], 0))
    grad_ref[:LEN, 2 * HD : 3 * HD] = (gv_ref[...] + received[:LEN, HD:]).astype(BF16)
    keys = unit_ref[:, HD : 2 * HD]
    reflect = unit_ref[:, 2 * HD :]
    reflect_s = split(reflect)
    y_s = split(y_ref[...])
    vb = vb_ref[...]
    vb_s = split(vb)
    beta_col = 2.0 * jax.nn.sigmoid(lcol_ref[...])
    beta_row = 2.0 * jax.nn.sigmoid(lrow_ref[...])
    row, col = rows_of(LEN), cols_of(LEN)
    on_keys = mxu(key_on_ref[...], d_keys, NN) + mxu(key_low_ref[...], d_keys, NN)
    side_k = three((fac_ref[...], fac_low_ref[...]), split(on_keys))
    side_q = taq_ref[...] + three(vb_s, d_map)
    dw = dw_ref[...] - side_k - three(y_s, d_map, NT) - beta_col * side_q
    d_system = low_ref[...] + three(split(side_q), y_s, NT) + three(vb_s, split(side_k), NT)
    d_system = jnp.where(row > col, d_system, 0.0)
    diagonal = scale_ref[:, HD - 1 :] + jnp.sum(
        side_q * reflect + vb * on_keys, axis=1, keepdims=True
    )
    gram = three(reflect_s, reflect_s, NT)
    d_beta = split(jnp.where(row == col, -diagonal, 0.0) + d_system * gram)
    ones = jnp.ones((TALL - LEN, LEN), BF16)
    d_beta = mxu(ones, d_beta[0], NT) + mxu(ones, d_beta[1], NT)
    d_logit = d_beta * beta_row * (1.0 - 0.5 * beta_row)
    first = lax.broadcasted_iota(jnp.int32, (TALL - LEN, LEN), 0) == 0
    grad_ref[LEN:] = jnp.where(first, d_logit, 0.0).astype(BF16)
    d_gram = split(beta_col * d_system)
    dw = dw + three(d_gram, reflect_s, NN)
    dw_t = three(reflect_s, d_gram, TN)
    d_key_on = beta_col * xtn_ref[...].astype(F32) + one(vt_ref[...], d_keys.T, TN)
    d_key_on = -jnp.where(row > col, d_key_on, 0.0)
    d_key_on = d_key_on.astype(BF16)
    dk_t = mxu(reflect_s[0], d_key_on, TN)
    dw = dw + one(d_key_on, keys, NN) + dw_t.T
    dk = d_keys.astype(F32) + dk_ref[...] + dk_t.T
    grad_ref[:LEN, :HD] = dq_ref[...]
    grad_ref[:LEN, HD : 2 * HD] = unit_back(dk, keys, scale_ref[:, :1]).astype(BF16)
    side = scale_ref[:, HD // 4 : HD // 4 + 1]
    grad_ref[:LEN, 3 * HD :] = unit_back(dw, reflect, side).astype(BF16)


def shape(*dims, dtype=F32):
    return jax.ShapeDtypeStruct(dims, dtype)


class Flow:
    def __init__(self, semaphores):
        self.semaphores = semaphores
        self.used = 0
        self.open = []

    def fetch(self, source, target):
        copy = pltpu.make_async_copy(source, target, self.semaphores.at[self.used])
        self.used += 1
        copy.start()
        return copy

    def send(self, source, target):
        self.open.append(self.fetch(source, target))

    def finish(self):
        for copy in self.open:
            copy.wait()


VMEM = pl.BlockSpec(memory_space=pltpu.VMEM)
SMEM = pl.BlockSpec(memory_space=pltpu.SMEM)
HBM = pl.BlockSpec(memory_space=pltpu.HBM)


class Late:
    def __init__(self, ref, copy):
        self.ref = ref
        self.copy = copy

    def __getitem__(self, index):
        if self.copy is not None:
            self.copy.wait()
            self.copy = None
        return self.ref[index]


class Early:
    def __init__(self, flow, ref, target):
        self.flow = flow
        self.ref = ref
        self.target = target

    def __setitem__(self, index, value):
        self.ref[index] = value
        self.flow.send(self.ref, self.target)


def build(kernel, outs, args, in_specs, out_specs, scratch, copies, limit=32):
    def body(*refs):
        kernel(Flow(refs[-1]), *refs[:-1])

    single = not isinstance(outs, list)
    if single:
        outs, out_specs = [outs], [out_specs]
    args = [
        pltpu.with_memory_space_constraint(arg, pltpu.HBM) if spec is HBM else arg
        for arg, spec in zip(args, in_specs)
    ]
    outs = [
        pltpu.HBM(out.shape, out.dtype) if spec is HBM else out
        for out, spec in zip(outs, out_specs)
    ]
    results = pl.pallas_call(
        body,
        out_shape=outs,
        in_specs=in_specs,
        out_specs=out_specs,
        scratch_shapes=list(scratch) + [pltpu.SemaphoreType.DMA((copies,))],
        compiler_params=pltpu.CompilerParams(vmem_limit_bytes=limit * 2**20),
        cost_estimate=pl.CostEstimate(
            flops=2 * 10**9, bytes_accessed=4 * 2**20, transcendentals=0
        ),
    )(*args)
    return results[0] if single else results


def call(kernel, outs, *args, far_in=(), far_out=(), limit=32):
    far_in, far_out = tuple(far_in), tuple(far_out)
    count = len(args)

    def body(flow, *refs):
        ins, results = list(refs[:count]), list(refs[count : count + len(outs)])
        buffers = list(refs[count + len(outs) :])
        for i in far_in:
            buffer = buffers.pop(0)
            ins[i] = Late(buffer, flow.fetch(ins[i], buffer))
        for i in far_out:
            results[i] = Early(flow, buffers.pop(0), results[i])
        kernel(*ins, *results)
        flow.finish()

    return build(
        body,
        outs,
        args,
        [HBM if i in far_in else VMEM for i in range(count)],
        [HBM if i in far_out else VMEM for i in range(len(outs))],
        [pltpu.VMEM(args[i].shape, args[i].dtype) for i in far_in]
        + [pltpu.VMEM(outs[i].shape, outs[i].dtype) for i in far_out],
        max(1, len(far_in) + len(far_out)),
        limit,
    )


def project_kernel(offsets):
    def body(flow, where_ref, bias_ref, own_ref, swap_ref, weight_hbm, beta_ref, *refs):
        later = len(refs) == 9
        before = refs[:3] if later else None
        all_hbm, proj_ref, col_ref, row_ref, all_ref, weight_ref = refs[-6:]
        my_z, my_y, my_core = where_ref[2], where_ref[3], where_ref[4]
        places = [lax.rem(my_z + offset + DEPTH, DEPTH) for offset in offsets]
        copies = [
            flow.fetch(weight_hbm.at[pl.ds(pl.multiple_of(z * LEN, LEN), LEN)], weight_ref.at[k])
            for k, z in enumerate(places)
        ]
        for k in range(len(offsets)):
            for side in range(2):
                base = 2 * (my_y if side == 0 else 1 - my_y)
                all_ref[k, base + my_core] = own_ref[k, side]
                all_ref[k, base + 1 - my_core] = swap_ref[k, side]
            flow.send(all_ref.at[k], all_hbm.at[k])
        proj = before[0][...] if later else jnp.zeros((LEN, 4 * HD), F32)
        col = before[1][...] if later else jnp.zeros((LEN, 8), F32) + bias_ref[0]
        row = before[2][...] if later else jnp.zeros((8, LEN), F32) + bias_ref[0]
        for k, z in enumerate(places):
            features = jnp.concatenate([all_ref[k, j] for j in range(4)], axis=1)
            beta = jnp.broadcast_to(beta_ref[z], (8, LEN)).astype(BF16)
            col = col + mxu(features, beta, NT)
            row = row + mxu(beta, features, NT)
            copies[k].wait()
            proj = proj + mxu(features, weight_ref[k], NN)
        proj_ref[...] = proj
        col_ref[...] = col
        row_ref[...] = row
        flow.finish()

    return body


def project(offsets, where, bias, own, swap, weights, betas, before=()):
    count = len(offsets)
    return build(
        project_kernel(offsets),
        [
            shape(count, 4, LEN, HD, dtype=BF16),
            shape(LEN, 4 * HD),
            shape(LEN, 8),
            shape(8, LEN),
        ],
        (where, bias, own, swap, weights, betas) + tuple(before),
        [SMEM, SMEM, VMEM, VMEM, HBM, VMEM] + [VMEM] * len(before),
        [HBM, VMEM, VMEM, VMEM],
        [
            pltpu.VMEM((count, 4, LEN, HD), BF16),
            pltpu.VMEM((count, LEN, 4 * HD), BF16),
        ],
        2 * count,
    )


def weight_kernel(columns, tail):
    def body(flow, where_ref, near_hbm, far_hbm, grad_ref, out_hbm, all_ref, out_ref):
        my_z = where_ref[2]
        copies = [
            flow.fetch(near_hbm.at[k] if k < 5 else far_hbm.at[k - 5], all_ref.at[k])
            for k in range(DEPTH)
        ]
        grad = grad_ref[:LEN, columns]
        for k, offset in enumerate(OFFSETS):
            copies[k].wait()
            features = jnp.concatenate([all_ref[k, j] for j in range(4)], axis=1)
            out_ref[k, :LEN] = mxu(features, grad, TN).astype(BF16)
            if tail:
                beta = mxu(grad_ref[LEN:], features, NN).astype(BF16)
                rest = jnp.zeros((TALL - LEN, 2 * HD), BF16)
                out_ref[k, LEN:TALL] = beta[:, : LEN - HD]
                out_ref[k, TALL:] = jnp.concatenate([beta[:, LEN - HD :], rest], axis=1)
            flow.send(out_ref.at[k], out_hbm.at[lax.rem(my_z + offset + DEPTH, DEPTH)])
        flow.finish()

    return body


def weight_sums(columns, tail, where, near_all, far_all, grad):
    rows, width = LEN + tail, columns.stop - columns.start
    terms = build(
        weight_kernel(columns, tail),
        shape(SHARDS, rows, width, dtype=BF16),
        (where, near_all, far_all, grad),
        [SMEM, HBM, HBM, VMEM],
        HBM,
        [pltpu.VMEM((DEPTH, 4, LEN, HD), BF16), pltpu.VMEM((SHARDS, rows, width), BF16)],
        2 * DEPTH,
    )
    return lax.all_to_all(terms, CTX, 0, 0)


def total_kernel(queries_ref, rest_ref, weight_ref, beta_ref):
    for ref, columns in ((queries_ref, slice(0, HD)), (rest_ref, slice(HD, 4 * HD))):
        total = ref[0, :LEN].astype(F32)
        for a in range(1, SHARDS):
            total = total + ref[a, :LEN].astype(F32)
        weight_ref[:, columns] = total.astype(BF16)
    beta = rest_ref[0, LEN:].astype(F32)
    for a in range(1, SHARDS):
        beta = beta + rest_ref[a, LEN:].astype(F32)
    extra = TALL - LEN
    beta_ref[...] = jnp.concatenate([beta[:1], beta[extra : extra + 1, :HD]], axis=1)


def feature_kernel(offsets):
    def body(
        flow, where_ref, own_ref, other_ref, weight_hbm, away_hbm, own_beta, other_beta, out_ref,
        weight_ref, away_ref,
    ):
        my_z, my_y, my_core = where_ref[2], where_ref[3], where_ref[4]
        extra = TALL - LEN
        places = [lax.rem(my_z + offset + DEPTH, DEPTH) for offset in offsets]
        copies = []
        for k, z in enumerate(places):
            base = pl.multiple_of(z * LEN + my_core * HD, HD)
            copies.append(
                [
                    flow.fetch(weight_hbm.at[pl.ds(base, HD)], weight_ref.at[k, :HD]),
                    flow.fetch(weight_hbm.at[pl.ds(base + HALF, HD)], weight_ref.at[k, HD:]),
                    flow.fetch(away_hbm.at[z], away_ref.at[k]),
                ]
            )
        own, other = own_ref[:LEN], other_ref[:LEN]
        logits = jnp.concatenate([own_ref[LEN:], other_ref[LEN:]], axis=0)
        for k, z in enumerate(places):
            betas = jnp.concatenate(
                [
                    jnp.broadcast_to(own_beta[z], (extra, HALF)),
                    jnp.broadcast_to(other_beta[z], (extra, HALF)),
                ],
                axis=0,
            ).astype(BF16)
            for copy in copies[k]:
                copy.wait()
            term = mxu(own, weight_ref[k], NT) + mxu(other, away_ref[k], NT)
            term = (term + mxu(logits, betas, TN)).astype(BF16)
            out_ref[k, my_y] = term[:, :HD]
            out_ref[k, 1 - my_y] = term[:, HD:]

    return body


def features(offsets, *args):
    count = len(offsets)
    return build(
        feature_kernel(offsets),
        shape(count, 2, LEN, HD, dtype=BF16),
        args,
        [SMEM, VMEM, VMEM, HBM, HBM, VMEM, VMEM],
        VMEM,
        [pltpu.VMEM((count, HALF, 4 * HD), BF16), pltpu.VMEM((count, HALF, 4 * HD), BF16)],
        3 * count,
    )


def swapped(value, axis):
    return lax.ppermute(value, axis, [(0, 1), (1, 0)])


def turned(value, axis, step):
    count = lax.axis_size(axis)
    return lax.ppermute(value, axis, [(i, (i + step) % count) for i in range(count)])


def plus(*terms):
    total = terms[0].astype(F32)
    for term in terms[1:]:
        total = total + term.astype(F32)
    return total


def line_of(block):
    left, right = turned(block, "x", 1), turned(block, "x", -1)
    return block, left, right, turned(left[:CUT], "x", 1), turned(right[CUT:], "x", -1)


def scatter_heads(at):
    up = turned(at(-4)[0], "z", 1)
    down = turned(at(-4)[1], "z", -1)
    up = jnp.stack([plus(at(3)[0], up).astype(BF16), at(3)[1]])
    down = jnp.stack([at(-3)[0], plus(at(-3)[1], down).astype(BF16)])
    for step in (2, 1):
        up = plus(turned(up, "z", 1), at(step)).astype(BF16)
        down = plus(turned(down, "z", -1), at(-step)).astype(BF16)
    total = plus(turned(up, "z", 1), turned(down, "z", -1), at(0))
    return total[0] + swapped(total[1].astype(BF16), "y_hi").astype(F32)


def on_device(layer_input, grad_core, w_in, beta_proj, beta_bias):
    where = jnp.stack([lax.axis_index(axis) for axis in CTX + HEAD]).astype(jnp.int32)
    core = lax.axis_index("core")
    betas = beta_proj[0].astype(F32).reshape(DEPTH, 1, LEN)
    beta_by_core = beta_proj[0].reshape(2 * DEPTH, 2, HD)
    own_beta = lax.dynamic_index_in_dim(beta_by_core, core, 1, False).reshape(DEPTH, 1, HALF)
    away_beta = lax.dynamic_index_in_dim(beta_by_core, 1 - core, 1, False)
    away_beta = swapped(away_beta.reshape(DEPTH, 1, HALF), "core").astype(F32)
    own_beta = own_beta.astype(F32)
    pair = jnp.stack([layer_input, swapped(layer_input, "y_hi")])
    up, down = turned(pair, "z", 1), turned(pair, "z", -1)
    weights = w_in.reshape(w_in.shape[0], 4 * HD)
    up, down, weights, where, betas, own_beta = lax.optimization_barrier(
        (up, down, weights, where, betas, own_beta)
    )
    up_two, down_two = turned(up, "z", 1), turned(down, "z", -1)
    by_core = weights.reshape(2 * DEPTH, 2, HD, 4 * HD)
    away = lax.dynamic_index_in_dim(by_core, 1 - core, 1, False).reshape(DEPTH, HALF, 4 * HD)
    up_two, down_two, away, away_beta = lax.optimization_barrier(
        (up_two, down_two, away, away_beta)
    )
    near = jnp.stack([pair, up, down, up_two, down_two])
    near_swap = swapped(near, "core")
    up_three, down_three = turned(up_two, "z", 1), turned(down_two, "z", -1)
    last = jnp.stack([turned(up_three[0], "z", 1), turned(down_three[1], "z", -1)])
    near_all, *partial = project(NEAR, where, beta_bias, near, near_swap, weights, betas)
    far = jnp.stack([up_three, down_three, last])
    far_swap = swapped(far, "core")
    far_all, projected, logit_col, logit_row = project(
        FAR, where, beta_bias, far, far_swap, weights, betas, partial
    )
    logit_col, logit_row = logit_col[:, :1], logit_row[:1]
    sent, inverse, unit, y_side, vt_side = call(
        first_kernel,
        [
            shape(PACK, HD, dtype=BF16),
            shape(LEN, LEN),
            shape(LEN, 3 * HD),
            shape(LEN, HD),
            shape(HD, LEN),
        ],
        projected,
        logit_col,
        logit_row,
        far_out=(1, 2, 3, 4),
    )
    square = shape(LEN, LEN, dtype=BF16)
    query_dev, ut_side, exp_in, query_on, query_low, key_on, key_low, total_in, acc_in = call(
        second_kernel,
        [shape(LEN, HD, dtype=BF16)] + [square] * 6 + [shape(1, LEN), shape(HD, LEN)],
        unit,
        inverse,
        logit_row,
        y_side,
        sent,
        far_in=(0, 1, 3),
        far_out=(1, 2, 3, 4, 5, 6),
    )
    other, query_dev = lax.optimization_barrier((swapped(sent, "y_lo"), query_dev))
    shards = line_of(sent) + line_of(other)
    back, grad_query, core_scaled, delta = build(
        third_kernel,
        [
            shape(SHARDS, LEN + HD // 2, 2 * HD, dtype=BF16),
            shape(HD, LEN),
            shape(LEN, HD, dtype=BF16),
            shape(1, LEN),
        ],
        (where, query_dev, *shards, grad_core, total_in, acc_in),
        [SMEM] + [VMEM] * 14,
        [HBM] * 4,
        [
            pltpu.VMEM((SHARDS - 1, LEN, LEN), BF16),
            pltpu.VMEM((SHARDS, PACK, HD), BF16),
            pltpu.VMEM((SHARDS, LEN + HD // 2, 2 * HD), BF16),
            pltpu.VMEM((HD, LEN), F32),
            pltpu.VMEM((LEN, HD), BF16),
            pltpu.VMEM((1, LEN), F32),
        ],
        SHARDS + 3,
    )
    returned = lax.all_to_all(back, CTX, 0, 0)
    away = swapped(away, "core")
    column = shape(LEN, HD)
    outs = call(
        fourth_kernel,
        [shape(LEN, HD, dtype=BF16)]
        + [column] * 5
        + [shape(LEN, LEN)]
        + [square] * 3
        + [column],
        projected,
        unit,
        inverse,
        logit_row,
        y_side,
        ut_side,
        exp_in,
        query_on,
        query_low,
        key_on,
        key_low,
        core_scaled,
        delta,
        grad_query,
        far_in=(0, 1, 2, 4, 5, 6, 7, 8, 9, 10, 11, 13),
        far_out=range(11),
    )
    dq, dk, dw, gv, taq, vb, low, xtn, factor, factor_low, scale = outs
    queries_w = weight_sums(slice(0, HD), 0, where, near_all, far_all, dq)
    grad_proj = call(
        fifth_kernel,
        [shape(TALL, 4 * HD, dtype=BF16)],
        unit,
        factor,
        factor_low,
        logit_col,
        logit_row,
        y_side,
        vt_side,
        key_on,
        key_low,
        dq,
        dk,
        dw,
        gv,
        taq,
        vb,
        low,
        xtn,
        scale,
        returned,
        far_in=(0, 1, 2) + tuple(range(5, 19)),
    )[0]
    other_proj = swapped(grad_proj, "core")
    sides = (where, grad_proj, other_proj, weights, away, own_beta, away_beta)
    first, second = (-4, 3, -3), (2, -2, 1, -1, 0)
    first_terms = features(first, *sides)
    second_terms = features(second, *sides)

    def at(offset):
        if offset in first:
            return first_terms[first.index(offset)]
        return second_terms[second.index(offset)]

    rest_w = weight_sums(slice(HD, 4 * HD), 32, where, near_all, far_all, grad_proj)
    grad_input = scatter_heads(at).astype(BF16)
    grad_w_in, grad_beta = call(
        total_kernel,
        [shape(LEN, 4 * HD, dtype=BF16), shape(1, 4 * HD)],
        queries_w,
        rest_w,
        far_in=(0, 1),
    )
    return (grad_input, grad_w_in.reshape(LEN, 1, 4, HD), grad_beta)


def solution(mesh):
    parts = Mesh(mesh.devices.reshape(2, WIDE, DEPTH, 2, 2), CTX + HEAD)
    in_specs = (P(CTX, HEAD), P(CTX, HEAD), P(None, HEAD, None, None), P(HEAD, None), P(HEAD))
    out_specs = (P(CTX, HEAD), P(CTX, HEAD, None, None), P(HEAD, CTX))
    return jax.shard_map(
        on_device, mesh=parts, in_specs=in_specs, out_specs=out_specs, check_vma=False
    )
```

```python
import jax
import jax.numpy as jnp
from jax import lax
from jax.experimental import pallas as pl
from jax.experimental.pallas import tpu as pltpu
from jax.sharding import Mesh
from jax.sharding import PartitionSpec as P

HD = 128
LEN = 512
HALF = 256
SHARDS = 8
CTX = ("y_lo", "x")
HEAD = ("z", "y_hi", "core")
DEPTH = 8
WIDE = 4
OFFSETS = (0, -1, 1, -2, 2, -3, 3, -4)
TALL = LEN + 16
NEAR = OFFSETS[:5]
FAR = OFFSETS[5:]
PACK = LEN + HD + LEN
CUT = PACK // 2
TEMP = 8.0
EPS = 1e-06
F32 = jnp.float32
BF16 = jnp.bfloat16
NN = ((1,), (0,))
NT = ((1,), (1,))
TN = ((0,), (0,))


def mxu(left, right, dims):
    return lax.dot_general(left, right, (dims, ((), ())), preferred_element_type=F32)


def one(left, right, dims=NN):
    return mxu(left.astype(BF16), right.astype(BF16), dims)


def split(matrix):
    high = matrix.astype(BF16)
    return high, (matrix - high.astype(F32)).astype(BF16)


def three(left, right, dims=NN):
    left_high, left_low = left
    right_high, right_low = right
    return (
        mxu(left_high, right_high, dims)
        + mxu(left_high, right_low, dims)
        + mxu(left_low, right_high, dims)
    )


def rows_of(size):
    return lax.broadcasted_iota(jnp.int32, (size, size), 0)


def cols_of(size):
    return lax.broadcasted_iota(jnp.int32, (size, size), 1)


def part(matrix, rows, cols):
    if isinstance(matrix, tuple):
        return tuple(half[rows, cols] for half in matrix)
    return matrix[rows, cols]


TOP = slice(0, HALF)
BOT = slice(HALF, LEN)
ALL = slice(0, LEN)


def lower_times_lower(left, right, product):
    top = product(part(left, TOP, TOP), part(right, TOP, TOP), NN)
    corner = product(part(left, BOT, ALL), part(right, ALL, TOP), NN)
    bottom = product(part(left, BOT, BOT), part(right, BOT, BOT), NN)
    zero = jnp.zeros((HALF, HALF), F32)
    return jnp.concatenate(
        [jnp.concatenate([top, zero], 1), jnp.concatenate([corner, bottom], 1)], 0
    )


def lower_times_upper_t(left, right, product):
    top = product(part(left, TOP, TOP), part(right, TOP, TOP), NT)
    corner = product(part(left, BOT, TOP), part(right, TOP, TOP), NT)
    bottom = product(part(left, BOT, ALL), part(right, BOT, ALL), NT)
    zero = jnp.zeros((HALF, HALF), F32)
    return jnp.concatenate(
        [jnp.concatenate([top, zero], 1), jnp.concatenate([corner, bottom], 1)], 0
    )


def upper_times_lower(left, right, product):
    top = product(part(left, TOP, ALL), part(right, ALL, TOP), NN)
    corner = product(part(left, BOT, BOT), part(right, BOT, TOP), NN)
    bottom = product(part(left, BOT, BOT), part(right, BOT, BOT), NN)
    zero = jnp.zeros((HALF, HALF), F32)
    return jnp.concatenate(
        [jnp.concatenate([top, zero], 1), jnp.concatenate([corner, bottom], 1)], 0
    )


def upper_times_upper(left, right, product, dims):
    if dims == NN:
        top = product(part(left, TOP, TOP), part(right, TOP, TOP), NN)
        corner = product(part(left, TOP, ALL), part(right, ALL, BOT), NN)
        bottom = product(part(left, BOT, BOT), part(right, BOT, BOT), NN)
    else:
        top = product(part(left, TOP, TOP), part(right, TOP, TOP), NT)
        corner = product(part(left, TOP, ALL), part(right, BOT, ALL), NT)
        bottom = product(part(left, BOT, BOT), part(right, BOT, BOT), NT)
    zero = jnp.zeros((HALF, HALF), F32)
    return jnp.concatenate(
        [jnp.concatenate([top, corner], 1), jnp.concatenate([zero, bottom], 1)], 0
    )


def unit_scale(matrix):
    return 1.0 / jnp.sqrt(jnp.sum(matrix * matrix, axis=1, keepdims=True) + EPS)


def inverse_blocks(blocks):
    size = HD
    row, col = rows_of(size), cols_of(size)
    found = []
    for block in blocks:
        first = ((row >> 1) == (col >> 1)) & (row > col)
        found.append(jnp.where(row == col, 1.0, 0.0) - jnp.where(first, block, 0.0))
    step = 1
    while (2 << step) <= size:
        pair = ((row >> (step + 1)) == (col >> (step + 1))) & ((row >> step) > (col >> step))
        halves = [split(inverse) for inverse in found]
        mixed = [
            split(three(split(jnp.where(pair, block, 0.0)), half))
            for block, half in zip(blocks, halves)
        ]
        found = [
            inverse - three(half, mix) for inverse, half, mix in zip(found, halves, mixed)
        ]
        step += 1
    return found


def first_kernel(
    proj_ref, lcol_ref, lrow_ref, pack_ref, inv_ref, unit_ref, y_ref, vt_ref,
    inv_near, unit_near, y_near,
):
    proj = proj_ref[...]
    keys_raw = proj[:, HD : 2 * HD]
    reflect_raw = proj[:, 3 * HD :]
    queries_raw = proj[:, :HD]
    queries = queries_raw * unit_scale(queries_raw)
    keys = keys_raw * unit_scale(keys_raw)
    reflect = reflect_raw * unit_scale(reflect_raw)
    unit_ref[...] = jnp.concatenate([queries, keys, reflect], axis=1)
    unit_near[...] = jnp.concatenate([queries, keys, reflect], axis=1)
    beta_col = 2.0 * jax.nn.sigmoid(lcol_ref[...])
    beta_row = 2.0 * jax.nn.sigmoid(lrow_ref[...])
    reflect_s = split(reflect)
    row, col = rows_of(HD), cols_of(HD)

    def system(i, j):
        rows, cols = slice(i * HD, (i + 1) * HD), slice(j * HD, (j + 1) * HD)
        gram = three(part(reflect_s, rows, slice(None)), part(reflect_s, cols, slice(None)), NT)
        gram = beta_col[rows] * gram
        return jnp.where(row > col, gram, 0.0) if i == j else gram

    solved = inverse_blocks([system(i, i) for i in range(4)])
    solved_s = [split(inverse) for inverse in solved]
    pairs = []
    for i in (0, 2):
        mix = three(split(system(i + 1, i)), solved_s[i])
        corner = -three(solved_s[i + 1], split(mix))
        zero = jnp.zeros((HD, HD), F32)
        pairs.append(
            jnp.concatenate(
                [
                    jnp.concatenate([solved[i], zero], 1),
                    jnp.concatenate([corner, solved[i + 1]], 1),
                ],
                0,
            )
        )
    top_s, bottom_s = split(pairs[0]), split(pairs[1])
    wide = three(part(reflect_s, BOT, slice(None)), part(reflect_s, TOP, slice(None)), NT)
    mix = three(split(beta_col[BOT] * wide), top_s)
    corner = -three(bottom_s, split(mix))
    zero = jnp.zeros((HALF, HALF), F32)
    whole = jnp.concatenate(
        [jnp.concatenate([pairs[0], zero], 1), jnp.concatenate([corner, pairs[1]], 1)], 0
    )
    inv_ref[...] = whole
    inv_near[...] = whole
    corner_s = split(corner)
    scaled_s = split(beta_col * reflect)
    y_top = three(top_s, part(scaled_s, TOP, slice(None)))
    y_bottom = three(corner_s, part(scaled_s, TOP, slice(None))) + three(
        bottom_s, part(scaled_s, BOT, slice(None))
    )
    y_all = jnp.concatenate([y_top, y_bottom], 0)
    y_ref[...] = y_all
    y_near[...] = y_all
    vt_top = three(part(reflect_s, TOP, slice(None)), top_s, TN) + three(
        part(reflect_s, BOT, slice(None)), corner_s, TN
    )
    vt_bottom = three(part(reflect_s, BOT, slice(None)), bottom_s, TN)
    vt_all = jnp.concatenate([vt_top, vt_bottom], 1) * beta_row
    vt_ref[...] = vt_all
    big_row, big_col = rows_of(LEN), cols_of(LEN)
    key_on = jnp.where(big_col > big_row, three(split(keys), reflect_s, NT), 0.0)
    pack_ref[:LEN] = (keys - three(split(key_on), split(vt_all), NT)).astype(BF16)
    change = jnp.where(row == col, 1.0, 0.0) - three(reflect_s, split(y_all), TN)
    pack_ref[LEN : LEN + HD] = change.astype(BF16)
    pack_ref[LEN + HD :] = proj[:, 2 * HD : 3 * HD].astype(BF16)


def second_kernel(
    unit_ref, inv_ref, lrow_ref, y_ref, v_ref,
    qd_ref, ut_ref, exp_ref, query_on_ref, query_low_ref, key_on_ref, key_low_ref, total_ref, acc_ref,
):
    queries = split(unit_ref[:, :HD])
    keys = split(unit_ref[:, HD : 2 * HD])
    reflect = split(unit_ref[:, 2 * HD :])
    beta_row = 2.0 * jax.nn.sigmoid(lrow_ref[...])
    row, col = rows_of(LEN), cols_of(LEN)
    query_on = jnp.where(row >= col, three(queries, reflect, NT), 0.0)
    qd_ref[...] = (
        TEMP * (unit_ref[:, :HD] - three(split(query_on), split(y_ref[...])))
    ).astype(BF16)
    query_on_t = jnp.where(row <= col, three(reflect, queries, NT), 0.0)
    query_on_t = split(query_on_t)
    query_on_ref[...] = query_on_t[0]
    query_low_ref[...] = query_on_t[1]
    key_on = jnp.where(row < col, three(keys, reflect, NT), 0.0)
    key_on_t = split(jnp.where(row > col, three(reflect, keys, NT), 0.0))
    key_on_ref[...] = key_on_t[0]
    key_low_ref[...] = key_on_t[1]
    factor = split(inv_ref[...] * beta_row)
    key_on = split(key_on)
    ut = split(upper_times_upper(key_on, factor, three, NT))
    ut_ref[...] = ut[0]
    scores = TEMP * (three(keys, queries, NT) - upper_times_upper(ut, query_on_t, three, NN))
    exped = jnp.where(row <= col, jnp.exp(scores), 0.0)
    total_ref[...] = jnp.sum(exped, axis=0, keepdims=True)
    exped = exped.astype(BF16)
    exp_ref[...] = exped
    acc_ref[...] = mxu(v_ref[LEN + HD :], exped, TN)


def third_kernel(
    flow, where_ref, qd_ref, own, own_left, own_right, own_far0, own_far1,
    other, other_left, other_right, other_far0, other_far1,
    core_ref, total_ref, acc_ref,
    out_hbm, grad_q_hbm, core_scaled_hbm, delta_hbm,
    exp_ref, keys_ref, out_ref, grad_q_ref, core_scaled_ref, delta_ref,
):
    my_y, my_x = where_ref[0], where_ref[1]
    me = my_y * WIDE + my_x
    for line, parts in (
        (my_y, (own, own_left, own_right, own_far0, own_far1)),
        (1 - my_y, (other, other_left, other_right, other_far0, other_far1)),
    ):
        for shift, part_ref in ((0, parts[0]), (-1, parts[1]), (1, parts[2])):
            keys_ref[line * WIDE + lax.rem(my_x + shift + WIDE, WIDE)] = part_ref[...]
        far = line * WIDE + lax.rem(my_x + 2, WIDE)
        keys_ref[far, :CUT] = parts[3][...]
        keys_ref[far, CUT:] = parts[4][...]
    queries = qd_ref[...]
    total = total_ref[...]
    acc = acc_ref[...]
    eye = jnp.where(rows_of(HD) == cols_of(HD), 1.0, 0.0).astype(BF16)
    carry = [None] * (SHARDS - 1)
    moved = [None] * (SHARDS - 1)

    def change_of(b):
        return keys_ref[b, LEN : LEN + HD]

    for b in range(SHARDS - 2, -1, -1):
        if b == SHARDS - 2:
            carry[b] = eye
        else:
            follow = mxu(carry[b + 1], change_of(b + 1), NN)
            carry[b] = jnp.where(b >= me - 1, eye.astype(F32), follow).astype(BF16)
        moved[b] = mxu(keys_ref[b, :LEN], carry[b], NT).astype(BF16)
        bias = jnp.where(b < me, 0.0, -1e30).astype(F32)
        exped = jnp.exp(mxu(moved[b], queries, NT) + bias)
        total = total + jnp.sum(exped, axis=0, keepdims=True)
        exped = exped.astype(BF16)
        exp_ref[b] = exped
        acc = acc + mxu(keys_ref[b, LEN + HD :], exped, TN)
    inverse_total = 1.0 / total
    core_t = core_ref[...].astype(F32).T
    delta = jnp.sum(core_t * acc, axis=0, keepdims=True) * inverse_total * inverse_total
    delta_ref[...] = delta
    core_t = core_t * inverse_total
    core_scaled = core_t.T.astype(BF16)
    core_scaled_ref[...] = core_scaled
    grad_q = jnp.zeros((HD, LEN), F32)
    inner = jnp.zeros((HD, HD), F32)
    out_ref[SHARDS - 1] = jnp.zeros(out_ref.shape[1:], BF16)
    flow.send(out_ref.at[SHARDS - 1], out_hbm.at[SHARDS - 1])
    flow.send(core_scaled_ref, core_scaled_hbm)
    flow.send(delta_ref, delta_hbm)
    for b in range(SHARDS - 1):
        keys = keys_ref[b, :LEN]
        exped = exp_ref[b]
        change = mxu(keys_ref[b, LEN + HD :], core_scaled, NT)
        grad_scores = (exped.astype(F32) * (change - delta)).astype(BF16)
        grad_q = grad_q + mxu(moved[b], grad_scores, TN)
        through = mxu(grad_scores, queries, NN).astype(BF16)
        out_ref[b, :LEN, :HD] = mxu(through, carry[b], NN).astype(BF16)
        out_ref[b, :LEN, HD:] = mxu(exped, core_scaled, NN).astype(BF16)
        if b >= 1:
            live = jnp.where(b < me, 1.0, 0.0).astype(F32)
            out_map = (one(carry[b], inner, TN) * live).astype(BF16)
        else:
            out_map = jnp.zeros((HD, HD), BF16)
        out_ref[b, LEN:, :HD] = out_map[: HD // 2]
        out_ref[b, LEN:, HD:] = out_map[HD // 2 :]
        flow.send(out_ref.at[b], out_hbm.at[b])
        if b < SHARDS - 2:
            step = mxu(through, keys, TN)
            inner = step if b == 0 else one(inner, change_of(b), NT) + step
    grad_q_ref[...] = TEMP * grad_q
    flow.send(grad_q_ref, grad_q_hbm)
    flow.finish()


def fourth_kernel(
    proj_ref, unit_ref, inv_ref, lrow_ref, y_ref, ut_ref, exp_ref, query_on_ref, query_low_ref,
    key_on_ref, key_low_ref, core_scaled_ref, delta_ref, grad_q_ref,
    dq_ref, dk_ref, dw_ref, gv_ref, taq_ref, vb_ref, low_ref, xtn_ref, fac_ref, fac_low_ref, scale_ref,
):
    queries = unit_ref[:, :HD].astype(BF16)
    keys = unit_ref[:, HD : 2 * HD].astype(BF16)
    reflect_s = split(unit_ref[:, 2 * HD :])
    reflect = reflect_s[0]
    beta_row = 2.0 * jax.nn.sigmoid(lrow_ref[...])
    row, col = rows_of(LEN), cols_of(LEN)
    core_scaled = core_scaled_ref[...]
    exped = exp_ref[...]
    gv_ref[...] = mxu(exped, core_scaled, NN)
    change = one(proj_ref[:, 2 * HD : 3 * HD], core_scaled, NT)
    grad_scores = (TEMP * exped.astype(F32) * (change - delta_ref[...])).astype(BF16)
    grad_q_t = grad_q_ref[...].astype(BF16)
    grad_q = grad_q_t.astype(F32).T.astype(BF16)
    query_on_t = query_on_ref[...]
    key_on_t = (key_on_ref[...], key_low_ref[...])
    inner = mxu(query_on_t, grad_scores, NT) + mxu(query_low_ref[...], grad_scores, NT)
    inner = split(jnp.where(row > col, inner, 0.0))
    side_q = mxu(query_on_t, grad_q, NN) + mxu(query_low_ref[...], grad_q, NN)
    inverse = inv_ref[...]
    factor = split(inverse * beta_row)
    fac_ref[...] = factor[0]
    fac_low_ref[...] = factor[1]
    inverse_t = split(inverse.T)
    taq_ref[...] = three(inverse_t, split(side_q))
    vb_ref[...] = three(inverse_t, reflect_s)
    mid = lower_times_upper_t(inner, key_on_t, three)
    mid = upper_times_lower(inverse_t, split(mid), three)
    low_ref[...] = lower_times_upper_t(split(mid), factor, three)
    diagonal = jnp.sum(jnp.where(row == col, mid, 0.0), axis=1, keepdims=True)
    xtn_ref[...] = upper_times_lower(inverse_t[0], inner[0], mxu).astype(BF16)
    d_query_on = mxu(ut_ref[...], grad_scores, TN) + one(y_ref[...], grad_q, NT)
    d_query_on = -jnp.where(row <= col, d_query_on, 0.0)
    d_query_on = d_query_on.astype(BF16)
    dq_t = grad_q_t.astype(F32) + mxu(keys, grad_scores, TN) + mxu(reflect, d_query_on, TN)
    scales = [unit_scale(proj_ref[:, k * HD : (k + 1) * HD]) for k in (0, 1, 3)]
    dq_ref[...] = unit_back(dq_t.T, unit_ref[:, :HD], scales[0]).astype(BF16)
    lane = lax.broadcasted_iota(jnp.int32, (LEN, HD), 1)
    scale_ref[...] = jnp.where(
        lane < HD // 4, scales[1], jnp.where(lane < HD // 2, scales[2], diagonal)
    )
    dw_ref[...] = mxu(d_query_on, queries, NN)
    dk_ref[...] = mxu(grad_scores, queries, NN)


def unit_back(grad, unit, scale):
    return (grad - unit * jnp.sum(unit * grad, axis=1, keepdims=True)) * scale


def fifth_kernel(
    unit_ref, fac_ref, fac_low_ref, lcol_ref, lrow_ref, y_ref, vt_ref, key_on_ref, key_low_ref,
    dq_ref, dk_ref, dw_ref, gv_ref, taq_ref, vb_ref, low_ref, xtn_ref, scale_ref, back_ref,
    grad_ref,
):
    received = back_ref[0].astype(F32)
    for a in range(1, SHARDS):
        received = received + back_ref[a].astype(F32)
    d_keys = received[:LEN, :HD].astype(BF16)
    d_map = split(jnp.concatenate([received[LEN:, :HD], received[LEN:, HD:]], 0))
    on_keys = mxu(key_on_ref[...], d_keys, NN) + mxu(key_low_ref[...], d_keys, NN)
    side_k = three((fac_ref[...], fac_low_ref[...]), split(on_keys))
    vb = vb_ref[...]
    vb_s = split(vb)
    side_q = taq_ref[...] + three(vb_s, d_map)
    beta_col = 2.0 * jax.nn.sigmoid(lcol_ref[...])
    beta_row = 2.0 * jax.nn.sigmoid(lrow_ref[...])
    row, col = rows_of(LEN), cols_of(LEN)
    y_s = split(y_ref[...])
    d_system = low_ref[...] + three(split(side_q), y_s, NT) + three(vb_s, split(side_k), NT)
    d_system = jnp.where(row > col, d_system, 0.0)
    dw = dw_ref[...] - side_k - three(y_s, d_map, NT) - beta_col * side_q
    keys = unit_ref[:, HD : 2 * HD]
    reflect = unit_ref[:, 2 * HD :]
    reflect_s = split(reflect)
    diagonal = scale_ref[:, HD - 1 :] + jnp.sum(
        side_q * reflect + vb * on_keys, axis=1, keepdims=True
    )
    gram = three(reflect_s, reflect_s, NT)
    d_beta = split(jnp.where(row == col, -diagonal, 0.0) + d_system * gram)
    ones = jnp.ones((TALL - LEN, LEN), BF16)
    d_beta = mxu(ones, d_beta[0], NT) + mxu(ones, d_beta[1], NT)
    d_logit = d_beta * beta_row * (1.0 - 0.5 * beta_row)
    first = lax.broadcasted_iota(jnp.int32, (TALL - LEN, LEN), 0) == 0
    grad_ref[LEN:] = jnp.where(first, d_logit, 0.0).astype(BF16)
    d_gram = split(beta_col * d_system)
    dw = dw + three(d_gram, reflect_s, NN)
    dw_t = three(reflect_s, d_gram, TN)
    d_key_on = beta_col * xtn_ref[...].astype(F32) + one(vt_ref[...], d_keys.T, TN)
    d_key_on = -jnp.where(row > col, d_key_on, 0.0)
    d_key_on = d_key_on.astype(BF16)
    dk_t = mxu(reflect_s[0], d_key_on, TN)
    dw = dw + one(d_key_on, keys, NN) + dw_t.T
    dk = d_keys.astype(F32) + dk_ref[...] + dk_t.T
    grad_ref[:LEN, 2 * HD : 3 * HD] = (gv_ref[...] + received[:LEN, HD:]).astype(BF16)
    grad_ref[:LEN, :HD] = dq_ref[...]
    grad_ref[:LEN, HD : 2 * HD] = unit_back(dk, keys, scale_ref[:, :1]).astype(BF16)
    side = scale_ref[:, HD // 4 : HD // 4 + 1]
    grad_ref[:LEN, 3 * HD :] = unit_back(dw, reflect, side).astype(BF16)


def shape(*dims, dtype=F32):
    return jax.ShapeDtypeStruct(dims, dtype)


class Flow:
    def __init__(self, semaphores):
        self.semaphores = semaphores
        self.used = 0
        self.open = []

    def fetch(self, source, target):
        copy = pltpu.make_async_copy(source, target, self.semaphores.at[self.used])
        self.used += 1
        copy.start()
        return copy

    def send(self, source, target):
        self.open.append(self.fetch(source, target))

    def finish(self):
        for copy in self.open:
            copy.wait()


VMEM = pl.BlockSpec(memory_space=pltpu.VMEM)
SMEM = pl.BlockSpec(memory_space=pltpu.SMEM)
HBM = pl.BlockSpec(memory_space=pltpu.HBM)


class Late:
    def __init__(self, ref, copy):
        self.ref = ref
        self.copy = copy

    def __getitem__(self, index):
        if self.copy is not None:
            self.copy.wait()
            self.copy = None
        return self.ref[index]


class Early:
    def __init__(self, flow, ref, target):
        self.flow = flow
        self.ref = ref
        self.target = target

    def __setitem__(self, index, value):
        self.ref[index] = value
        self.flow.send(self.ref, self.target)


def build(kernel, outs, args, in_specs, out_specs, scratch, copies, limit=32):
    def body(*refs):
        kernel(Flow(refs[-1]), *refs[:-1])

    single = not isinstance(outs, list)
    if single:
        outs, out_specs = [outs], [out_specs]
    args = [
        pltpu.with_memory_space_constraint(arg, pltpu.HBM) if spec is HBM else arg
        for arg, spec in zip(args, in_specs)
    ]
    outs = [
        pltpu.HBM(out.shape, out.dtype) if spec is HBM else out
        for out, spec in zip(outs, out_specs)
    ]
    results = pl.pallas_call(
        body,
        out_shape=outs,
        in_specs=in_specs,
        out_specs=out_specs,
        scratch_shapes=list(scratch) + [pltpu.SemaphoreType.DMA((copies,))],
        compiler_params=pltpu.CompilerParams(vmem_limit_bytes=limit * 2**20),
        cost_estimate=pl.CostEstimate(
            flops=2 * 10**9, bytes_accessed=4 * 2**20, transcendentals=0
        ),
    )(*args)
    return results[0] if single else results


def call(kernel, outs, *args, far_in=(), far_out=(), limit=32):
    far_in, far_out = tuple(far_in), tuple(far_out)
    count = len(args)

    def body(flow, *refs):
        ins, results = list(refs[:count]), list(refs[count : count + len(outs)])
        buffers = list(refs[count + len(outs) :])
        for i in far_in:
            buffer = buffers.pop(0)
            ins[i] = Late(buffer, flow.fetch(ins[i], buffer))
        for i in far_out:
            results[i] = Early(flow, buffers.pop(0), results[i])
        kernel(*ins, *results)
        flow.finish()

    return build(
        body,
        outs,
        args,
        [HBM if i in far_in else VMEM for i in range(count)],
        [HBM if i in far_out else VMEM for i in range(len(outs))],
        [pltpu.VMEM(args[i].shape, args[i].dtype) for i in far_in]
        + [pltpu.VMEM(outs[i].shape, outs[i].dtype) for i in far_out],
        max(1, len(far_in) + len(far_out)),
        limit,
    )


def project_kernel(offsets):
    def body(flow, where_ref, bias_ref, own_ref, swap_ref, weight_hbm, beta_ref, *refs):
        later = len(refs) == 9
        before = refs[:3] if later else None
        all_hbm, proj_ref, col_ref, row_ref, all_ref, weight_ref = refs[-6:]
        my_z, my_y, my_core = where_ref[2], where_ref[3], where_ref[4]
        places = [lax.rem(my_z + offset + DEPTH, DEPTH) for offset in offsets]
        copies = [
            flow.fetch(weight_hbm.at[pl.ds(pl.multiple_of(z * LEN, LEN), LEN)], weight_ref.at[k])
            for k, z in enumerate(places)
        ]
        for k in range(len(offsets)):
            for side in range(2):
                base = 2 * (my_y if side == 0 else 1 - my_y)
                all_ref[k, base + my_core] = own_ref[k, side]
                all_ref[k, base + 1 - my_core] = swap_ref[k, side]
            flow.send(all_ref.at[k], all_hbm.at[k])
        proj = before[0][...] if later else jnp.zeros((LEN, 4 * HD), F32)
        col = before[1][...] if later else jnp.zeros((LEN, 8), F32) + bias_ref[0]
        row = before[2][...] if later else jnp.zeros((8, LEN), F32) + bias_ref[0]
        for k, z in enumerate(places):
            features = jnp.concatenate([all_ref[k, j] for j in range(4)], axis=1)
            beta = jnp.broadcast_to(beta_ref[z], (8, LEN)).astype(BF16)
            col = col + mxu(features, beta, NT)
            row = row + mxu(beta, features, NT)
            copies[k].wait()
            proj = proj + mxu(features, weight_ref[k], NN)
        proj_ref[...] = proj
        col_ref[...] = col
        row_ref[...] = row
        flow.finish()

    return body


def project(offsets, where, bias, own, swap, weights, betas, before=()):
    count = len(offsets)
    return build(
        project_kernel(offsets),
        [
            shape(count, 4, LEN, HD, dtype=BF16),
            shape(LEN, 4 * HD),
            shape(LEN, 8),
            shape(8, LEN),
        ],
        (where, bias, own, swap, weights, betas) + tuple(before),
        [SMEM, SMEM, VMEM, VMEM, HBM, VMEM] + [VMEM] * len(before),
        [HBM, VMEM, VMEM, VMEM],
        [
            pltpu.VMEM((count, 4, LEN, HD), BF16),
            pltpu.VMEM((count, LEN, 4 * HD), BF16),
        ],
        2 * count,
    )


def weight_kernel(columns, tail):
    def body(flow, where_ref, near_hbm, far_hbm, grad_ref, out_hbm, all_ref, out_ref):
        my_z = where_ref[2]
        copies = [
            flow.fetch(near_hbm.at[k] if k < 5 else far_hbm.at[k - 5], all_ref.at[k])
            for k in range(DEPTH)
        ]
        grad = grad_ref[:LEN, columns]
        for k, offset in enumerate(OFFSETS):
            copies[k].wait()
            features = jnp.concatenate([all_ref[k, j] for j in range(4)], axis=1)
            out_ref[k, :LEN] = mxu(features, grad, TN).astype(BF16)
            if tail:
                beta = mxu(grad_ref[LEN:], features, NN).astype(BF16)
                rest = jnp.zeros((TALL - LEN, 2 * HD), BF16)
                out_ref[k, LEN:TALL] = beta[:, : LEN - HD]
                out_ref[k, TALL:] = jnp.concatenate([beta[:, LEN - HD :], rest], axis=1)
            flow.send(out_ref.at[k], out_hbm.at[lax.rem(my_z + offset + DEPTH, DEPTH)])
        flow.finish()

    return body


def weight_sums(columns, tail, where, near_all, far_all, grad):
    rows, width = LEN + tail, columns.stop - columns.start
    terms = build(
        weight_kernel(columns, tail),
        shape(SHARDS, rows, width, dtype=BF16),
        (where, near_all, far_all, grad),
        [SMEM, HBM, HBM, VMEM],
        HBM,
        [pltpu.VMEM((DEPTH, 4, LEN, HD), BF16), pltpu.VMEM((SHARDS, rows, width), BF16)],
        2 * DEPTH,
    )
    return terms


def total_kernel(queries_ref, rest_ref, weight_ref, beta_ref):
    for ref, columns in ((queries_ref, slice(0, HD)), (rest_ref, slice(HD, 4 * HD))):
        total = ref[0, :LEN].astype(F32)
        for a in range(1, SHARDS):
            total = total + ref[a, :LEN].astype(F32)
        weight_ref[:, columns] = total.astype(BF16)
    beta = rest_ref[0, LEN:].astype(F32)
    for a in range(1, SHARDS):
        beta = beta + rest_ref[a, LEN:].astype(F32)
    extra = TALL - LEN
    beta_ref[...] = jnp.concatenate([beta[:1], beta[extra : extra + 1, :HD]], axis=1)


def feature_kernel(offsets):
    def body(
        flow, where_ref, own_ref, other_ref, weight_hbm, away_hbm, own_beta, other_beta, out_ref,
        weight_ref, away_ref,
    ):
        my_z, my_y, my_core = where_ref[2], where_ref[3], where_ref[4]
        extra = TALL - LEN
        places = [lax.rem(my_z + offset + DEPTH, DEPTH) for offset in offsets]
        copies = []
        for k, z in enumerate(places):
            base = pl.multiple_of(z * LEN + my_core * HD, HD)
            copies.append(
                [
                    flow.fetch(weight_hbm.at[pl.ds(base, HD)], weight_ref.at[k, :HD]),
                    flow.fetch(weight_hbm.at[pl.ds(base + HALF, HD)], weight_ref.at[k, HD:]),
                    flow.fetch(away_hbm.at[z], away_ref.at[k]),
                ]
            )
        own, other = own_ref[:LEN], other_ref[:LEN]
        logits = jnp.concatenate([own_ref[LEN:], other_ref[LEN:]], axis=0)
        for k, z in enumerate(places):
            betas = jnp.concatenate(
                [
                    jnp.broadcast_to(own_beta[z], (extra, HALF)),
                    jnp.broadcast_to(other_beta[z], (extra, HALF)),
                ],
                axis=0,
            ).astype(BF16)
            for copy in copies[k]:
                copy.wait()
            term = mxu(own, weight_ref[k], NT) + mxu(other, away_ref[k], NT)
            term = (term + mxu(logits, betas, TN)).astype(BF16)
            out_ref[k, my_y] = term[:, :HD]
            out_ref[k, 1 - my_y] = term[:, HD:]

    return body


def features(offsets, *args):
    count = len(offsets)
    return build(
        feature_kernel(offsets),
        shape(count, 2, LEN, HD, dtype=BF16),
        args,
        [SMEM, VMEM, VMEM, HBM, HBM, VMEM, VMEM],
        VMEM,
        [pltpu.VMEM((count, HALF, 4 * HD), BF16), pltpu.VMEM((count, HALF, 4 * HD), BF16)],
        3 * count,
    )


def swapped(value, axis):
    return lax.ppermute(value, axis, [(0, 1), (1, 0)])


def turned(value, axis, step):
    count = lax.axis_size(axis)
    return lax.ppermute(value, axis, [(i, (i + step) % count) for i in range(count)])


def plus(*terms):
    total = terms[0].astype(F32)
    for term in terms[1:]:
        total = total + term.astype(F32)
    return total


def line_of(block):
    left, right = turned(block, "x", 1), turned(block, "x", -1)
    return block, left, right, turned(left[:CUT], "x", 1), turned(right[CUT:], "x", -1)


def scatter_heads(at, beside):
    up = turned(at(-4)[0], "z", 1)
    down = turned(at(-4)[1], "z", -1)
    up = jnp.stack([plus(at(3)[0], up).astype(BF16), at(3)[1]])
    down = jnp.stack([at(-3)[0], plus(at(-3)[1], down).astype(BF16)])
    for step in (2, 1):
        up = plus(turned(up, "z", 1), at(step)).astype(BF16)
        down = plus(turned(down, "z", -1), at(-step)).astype(BF16)
    total = plus(turned(up, "z", 1), turned(down, "z", -1), at(0))
    received, beside = lax.optimization_barrier(
        (swapped(total[1].astype(BF16), "y_hi"), beside)
    )
    return total[0] + received.astype(F32), beside


def on_device(layer_input, grad_core, w_in, beta_proj, beta_bias):
    where = jnp.stack([lax.axis_index(axis) for axis in CTX + HEAD]).astype(jnp.int32)
    core = lax.axis_index("core")
    betas = beta_proj[0].astype(F32).reshape(DEPTH, 1, LEN)
    beta_by_core = beta_proj[0].reshape(2 * DEPTH, 2, HD)
    own_beta = lax.dynamic_index_in_dim(beta_by_core, core, 1, False).reshape(DEPTH, 1, HALF)
    away_beta = lax.dynamic_index_in_dim(beta_by_core, 1 - core, 1, False)
    away_beta = swapped(away_beta.reshape(DEPTH, 1, HALF), "core").astype(F32)
    own_beta = own_beta.astype(F32)
    pair = jnp.stack([layer_input, swapped(layer_input, "y_hi")])
    up, down = turned(pair, "z", 1), turned(pair, "z", -1)
    weights = w_in.reshape(w_in.shape[0], 4 * HD)
    up, down, weights, where, betas, own_beta = lax.optimization_barrier(
        (up, down, weights, where, betas, own_beta)
    )
    up_two, down_two = turned(up, "z", 1), turned(down, "z", -1)
    by_core = weights.reshape(2 * DEPTH, 2, HD, 4 * HD)
    away = lax.dynamic_index_in_dim(by_core, 1 - core, 1, False).reshape(DEPTH, HALF, 4 * HD)
    up_two, down_two, away, away_beta = lax.optimization_barrier(
        (up_two, down_two, away, away_beta)
    )
    near = jnp.stack([pair, up, down, up_two, down_two])
    near_swap = swapped(near, "core")
    up_three, down_three = turned(up_two, "z", 1), turned(down_two, "z", -1)
    last = jnp.stack([turned(up_three[0], "z", 1), turned(down_three[1], "z", -1)])
    near_all, *partial = project(NEAR, where, beta_bias, near, near_swap, weights, betas)
    far = jnp.stack([up_three, down_three, last])
    far_swap = swapped(far, "core")
    far_all, projected, logit_col, logit_row = project(
        FAR, where, beta_bias, far, far_swap, weights, betas, partial
    )
    logit_col, logit_row = logit_col[:, :1], logit_row[:1]
    sent, inverse, unit, y_side, vt_side, *twins = call(
        first_kernel,
        [
            shape(PACK, HD, dtype=BF16),
            shape(LEN, LEN),
            shape(LEN, 3 * HD),
            shape(LEN, HD),
            shape(HD, LEN),
            shape(LEN, LEN),
            shape(LEN, 3 * HD),
            shape(LEN, HD),
        ],
        projected,
        logit_col,
        logit_row,
        far_out=(1, 2, 3, 4),
    )
    square = shape(LEN, LEN, dtype=BF16)
    query_dev, ut_side, exp_in, query_on, query_low, key_on, key_low, total_in, acc_in = call(
        second_kernel,
        [shape(LEN, HD, dtype=BF16)] + [square] * 6 + [shape(1, LEN), shape(HD, LEN)],
        twins[1],
        twins[0],
        logit_row,
        twins[2],
        sent,
        far_out=(1, 2, 3, 4, 5, 6),
    )
    other, query_dev = lax.optimization_barrier((swapped(sent, "y_lo"), query_dev))
    shards = line_of(sent) + line_of(other)
    back, grad_query, core_scaled, delta = build(
        third_kernel,
        [
            shape(SHARDS, LEN + HD // 2, 2 * HD, dtype=BF16),
            shape(HD, LEN),
            shape(LEN, HD, dtype=BF16),
            shape(1, LEN),
        ],
        (where, query_dev, *shards, grad_core, total_in, acc_in),
        [SMEM] + [VMEM] * 14,
        [HBM] * 4,
        [
            pltpu.VMEM((SHARDS - 1, LEN, LEN), BF16),
            pltpu.VMEM((SHARDS, PACK, HD), BF16),
            pltpu.VMEM((SHARDS, LEN + HD // 2, 2 * HD), BF16),
            pltpu.VMEM((HD, LEN), F32),
            pltpu.VMEM((LEN, HD), BF16),
            pltpu.VMEM((1, LEN), F32),
        ],
        SHARDS + 3,
    )
    returned = lax.all_to_all(back, CTX, 0, 0)
    away = swapped(away, "core")
    column = shape(LEN, HD)
    outs = call(
        fourth_kernel,
        [shape(LEN, HD, dtype=BF16)]
        + [column] * 5
        + [shape(LEN, LEN)]
        + [square] * 3
        + [column],
        projected,
        unit,
        inverse,
        logit_row,
        y_side,
        ut_side,
        exp_in,
        query_on,
        query_low,
        key_on,
        key_low,
        core_scaled,
        delta,
        grad_query,
        far_in=(0, 1, 2, 4, 5, 6, 7, 8, 9, 10, 11, 13),
        far_out=range(11),
    )
    dq, dk, dw, gv, taq, vb, low, xtn, factor, factor_low, scale = outs
    queries_w = weight_sums(slice(0, HD), 0, where, near_all, far_all, dq)
    returned, queries_w = lax.optimization_barrier((returned, queries_w))
    queries_w = lax.all_to_all(queries_w, CTX, 0, 0)
    grad_proj = call(
        fifth_kernel,
        [shape(TALL, 4 * HD, dtype=BF16)],
        unit,
        factor,
        factor_low,
        logit_col,
        logit_row,
        y_side,
        vt_side,
        key_on,
        key_low,
        dq,
        dk,
        dw,
        gv,
        taq,
        vb,
        low,
        xtn,
        scale,
        returned,
        far_in=(7, 8, 1, 2, 13, 14, 5, 15, 11, 0, 16, 6, 10, 17, 12, 9),
    )[0]
    other_proj = swapped(grad_proj, "core")
    sides = (where, grad_proj, other_proj, weights, away, own_beta, away_beta)
    first, second = (-4, 3, -3, 2, -2), (1, -1, 0)
    first_terms = features(first, *sides)
    second_terms = features(second, *sides)

    def at(offset):
        if offset in first:
            return first_terms[first.index(offset)]
        return second_terms[second.index(offset)]

    rest_w = weight_sums(slice(HD, 4 * HD), 32, where, near_all, far_all, grad_proj)
    rest_w = lax.all_to_all(rest_w, CTX, 0, 0)
    grad_w_in, grad_beta = call(
        total_kernel,
        [shape(LEN, 4 * HD, dtype=BF16), shape(1, 4 * HD)],
        queries_w,
        rest_w,
        far_in=(0, 1),
    )
    grad_input, (grad_w_in, grad_beta) = scatter_heads(
        at, (grad_w_in.reshape(LEN, 1, 4, HD), grad_beta)
    )
    return (grad_input.astype(BF16), grad_w_in, grad_beta)


def solution(mesh):
    parts = Mesh(mesh.devices.reshape(2, WIDE, DEPTH, 2, 2), CTX + HEAD)
    in_specs = (P(CTX, HEAD), P(CTX, HEAD), P(None, HEAD, None, None), P(HEAD, None), P(HEAD))
    out_specs = (P(CTX, HEAD), P(CTX, HEAD, None, None), P(HEAD, CTX))
    return jax.shard_map(
        on_device, mesh=parts, in_specs=in_specs, out_specs=out_specs, check_vma=False
    )
```

```python
import jax
import jax.numpy as jnp
from jax import lax
from jax.experimental import pallas as pl
from jax.experimental.pallas import tpu as pltpu
from jax.sharding import Mesh
from jax.sharding import PartitionSpec as P

HD = 128
LEN = 512
HALF = 256
SHARDS = 8
CTX = ("y_lo", "x")
HEAD = ("z", "y_hi", "core")
DEPTH = 8
WIDE = 4
OFFSETS = (0, -1, 1, -2, 2, -3, 3, -4)
TALL = LEN + 16
NEAR = OFFSETS[:5]
FAR = OFFSETS[5:]
PACK = LEN + HD + LEN
CUT = PACK // 2
TEMP = 8.0
EPS = 1e-06
F32 = jnp.float32
BF16 = jnp.bfloat16
NN = ((1,), (0,))
NT = ((1,), (1,))
TN = ((0,), (0,))


def mxu(left, right, dims):
    return lax.dot_general(left, right, (dims, ((), ())), preferred_element_type=F32)


def one(left, right, dims=NN):
    return mxu(left.astype(BF16), right.astype(BF16), dims)


def split(matrix):
    high = matrix.astype(BF16)
    return high, (matrix - high.astype(F32)).astype(BF16)


def three(left, right, dims=NN):
    left_high, left_low = left
    right_high, right_low = right
    return (
        mxu(left_high, right_high, dims)
        + mxu(left_high, right_low, dims)
        + mxu(left_low, right_high, dims)
    )


def rows_of(size):
    return lax.broadcasted_iota(jnp.int32, (size, size), 0)


def cols_of(size):
    return lax.broadcasted_iota(jnp.int32, (size, size), 1)


def part(matrix, rows, cols):
    if isinstance(matrix, tuple):
        return tuple(half[rows, cols] for half in matrix)
    return matrix[rows, cols]


TOP = slice(0, HALF)
BOT = slice(HALF, LEN)
ALL = slice(0, LEN)


def lower_times_lower(left, right, product):
    top = product(part(left, TOP, TOP), part(right, TOP, TOP), NN)
    corner = product(part(left, BOT, ALL), part(right, ALL, TOP), NN)
    bottom = product(part(left, BOT, BOT), part(right, BOT, BOT), NN)
    zero = jnp.zeros((HALF, HALF), F32)
    return jnp.concatenate(
        [jnp.concatenate([top, zero], 1), jnp.concatenate([corner, bottom], 1)], 0
    )


def lower_times_upper_t(left, right, product):
    top = product(part(left, TOP, TOP), part(right, TOP, TOP), NT)
    corner = product(part(left, BOT, TOP), part(right, TOP, TOP), NT)
    bottom = product(part(left, BOT, ALL), part(right, BOT, ALL), NT)
    zero = jnp.zeros((HALF, HALF), F32)
    return jnp.concatenate(
        [jnp.concatenate([top, zero], 1), jnp.concatenate([corner, bottom], 1)], 0
    )


def upper_times_lower(left, right, product):
    top = product(part(left, TOP, ALL), part(right, ALL, TOP), NN)
    corner = product(part(left, BOT, BOT), part(right, BOT, TOP), NN)
    bottom = product(part(left, BOT, BOT), part(right, BOT, BOT), NN)
    zero = jnp.zeros((HALF, HALF), F32)
    return jnp.concatenate(
        [jnp.concatenate([top, zero], 1), jnp.concatenate([corner, bottom], 1)], 0
    )


def upper_times_upper(left, right, product, dims):
    if dims == NN:
        top = product(part(left, TOP, TOP), part(right, TOP, TOP), NN)
        corner = product(part(left, TOP, ALL), part(right, ALL, BOT), NN)
        bottom = product(part(left, BOT, BOT), part(right, BOT, BOT), NN)
    else:
        top = product(part(left, TOP, TOP), part(right, TOP, TOP), NT)
        corner = product(part(left, TOP, ALL), part(right, BOT, ALL), NT)
        bottom = product(part(left, BOT, BOT), part(right, BOT, BOT), NT)
    zero = jnp.zeros((HALF, HALF), F32)
    return jnp.concatenate(
        [jnp.concatenate([top, corner], 1), jnp.concatenate([zero, bottom], 1)], 0
    )


def unit_scale(matrix):
    return 1.0 / jnp.sqrt(jnp.sum(matrix * matrix, axis=1, keepdims=True) + EPS)


def inverse_blocks(blocks):
    size = HD
    row, col = rows_of(size), cols_of(size)
    found = []
    for block in blocks:
        first = ((row >> 1) == (col >> 1)) & (row > col)
        found.append(jnp.where(row == col, 1.0, 0.0) - jnp.where(first, block, 0.0))
    step = 1
    while (2 << step) <= size:
        pair = ((row >> (step + 1)) == (col >> (step + 1))) & ((row >> step) > (col >> step))
        halves = [split(inverse) for inverse in found]
        mixed = [
            split(three(split(jnp.where(pair, block, 0.0)), half))
            for block, half in zip(blocks, halves)
        ]
        found = [
            inverse - three(half, mix) for inverse, half, mix in zip(found, halves, mixed)
        ]
        step += 1
    return found


def first_kernel(
    proj_ref, lcol_ref, lrow_ref, pack_ref, inv_ref, unit_ref, y_ref, vt_ref,
    inv_near, unit_near, y_near,
):
    proj = proj_ref[...]
    keys_raw = proj[:, HD : 2 * HD]
    reflect_raw = proj[:, 3 * HD :]
    queries_raw = proj[:, :HD]
    queries = queries_raw * unit_scale(queries_raw)
    keys = keys_raw * unit_scale(keys_raw)
    reflect = reflect_raw * unit_scale(reflect_raw)
    unit_ref[...] = jnp.concatenate([queries, keys, reflect], axis=1)
    unit_near[...] = jnp.concatenate([queries, keys, reflect], axis=1)
    beta_col = 2.0 * jax.nn.sigmoid(lcol_ref[...])
    beta_row = 2.0 * jax.nn.sigmoid(lrow_ref[...])
    reflect_s = split(reflect)
    row, col = rows_of(HD), cols_of(HD)

    def system(i, j):
        rows, cols = slice(i * HD, (i + 1) * HD), slice(j * HD, (j + 1) * HD)
        gram = three(part(reflect_s, rows, slice(None)), part(reflect_s, cols, slice(None)), NT)
        gram = beta_col[rows] * gram
        return jnp.where(row > col, gram, 0.0) if i == j else gram

    solved = inverse_blocks([system(i, i) for i in range(4)])
    solved_s = [split(inverse) for inverse in solved]
    pairs = []
    for i in (0, 2):
        mix = three(split(system(i + 1, i)), solved_s[i])
        corner = -three(solved_s[i + 1], split(mix))
        zero = jnp.zeros((HD, HD), F32)
        pairs.append(
            jnp.concatenate(
                [
                    jnp.concatenate([solved[i], zero], 1),
                    jnp.concatenate([corner, solved[i + 1]], 1),
                ],
                0,
            )
        )
    top_s, bottom_s = split(pairs[0]), split(pairs[1])
    wide = three(part(reflect_s, BOT, slice(None)), part(reflect_s, TOP, slice(None)), NT)
    mix = three(split(beta_col[BOT] * wide), top_s)
    corner = -three(bottom_s, split(mix))
    zero = jnp.zeros((HALF, HALF), F32)
    whole = jnp.concatenate(
        [jnp.concatenate([pairs[0], zero], 1), jnp.concatenate([corner, pairs[1]], 1)], 0
    )
    inv_ref[...] = whole
    inv_near[...] = whole
    corner_s = split(corner)
    scaled_s = split(beta_col * reflect)
    y_top = three(top_s, part(scaled_s, TOP, slice(None)))
    y_bottom = three(corner_s, part(scaled_s, TOP, slice(None))) + three(
        bottom_s, part(scaled_s, BOT, slice(None))
    )
    y_all = jnp.concatenate([y_top, y_bottom], 0)
    y_ref[...] = y_all
    y_near[...] = y_all
    vt_top = three(part(reflect_s, TOP, slice(None)), top_s, TN) + three(
        part(reflect_s, BOT, slice(None)), corner_s, TN
    )
    vt_bottom = three(part(reflect_s, BOT, slice(None)), bottom_s, TN)
    vt_all = jnp.concatenate([vt_top, vt_bottom], 1) * beta_row
    vt_ref[...] = vt_all
    big_row, big_col = rows_of(LEN), cols_of(LEN)
    key_on = jnp.where(big_col > big_row, three(split(keys), reflect_s, NT), 0.0)
    pack_ref[:LEN] = (keys - three(split(key_on), split(vt_all), NT)).astype(BF16)
    change = jnp.where(row == col, 1.0, 0.0) - three(reflect_s, split(y_all), TN)
    pack_ref[LEN : LEN + HD] = change.astype(BF16)
    pack_ref[LEN + HD :] = proj[:, 2 * HD : 3 * HD].astype(BF16)


def second_kernel(
    unit_ref, inv_ref, lrow_ref, y_ref, v_ref,
    qd_ref, ut_ref, exp_ref, query_on_ref, query_low_ref, key_on_ref, key_low_ref, total_ref, acc_ref,
):
    queries = split(unit_ref[:, :HD])
    keys = split(unit_ref[:, HD : 2 * HD])
    reflect = split(unit_ref[:, 2 * HD :])
    beta_row = 2.0 * jax.nn.sigmoid(lrow_ref[...])
    row, col = rows_of(LEN), cols_of(LEN)
    query_on = jnp.where(row >= col, three(queries, reflect, NT), 0.0)
    qd_ref[...] = (
        TEMP * (unit_ref[:, :HD] - three(split(query_on), split(y_ref[...])))
    ).astype(BF16)
    query_on_t = jnp.where(row <= col, three(reflect, queries, NT), 0.0)
    query_on_t = split(query_on_t)
    query_on_ref[...] = query_on_t[0]
    query_low_ref[...] = query_on_t[1]
    key_on = jnp.where(row < col, three(keys, reflect, NT), 0.0)
    key_on_t = split(jnp.where(row > col, three(reflect, keys, NT), 0.0))
    key_on_ref[...] = key_on_t[0]
    key_low_ref[...] = key_on_t[1]
    factor = split(inv_ref[...] * beta_row)
    key_on = split(key_on)
    ut = split(upper_times_upper(key_on, factor, three, NT))
    ut_ref[...] = ut[0]
    scores = TEMP * (three(keys, queries, NT) - upper_times_upper(ut, query_on_t, three, NN))
    exped = jnp.where(row <= col, jnp.exp(scores), 0.0)
    total_ref[...] = jnp.sum(exped, axis=0, keepdims=True)
    exped = exped.astype(BF16)
    exp_ref[...] = exped
    acc_ref[...] = mxu(v_ref[LEN + HD :], exped, TN)


def third_kernel(
    flow, where_ref, qd_ref, own, own_left, own_right, own_far0, own_far1,
    other, other_left, other_right, other_far0, other_far1,
    core_ref, total_ref, acc_ref,
    out_hbm, grad_q_hbm, core_scaled_hbm, delta_hbm,
    exp_ref, keys_ref, out_ref, grad_q_ref, core_scaled_ref, delta_ref,
):
    my_y, my_x = where_ref[0], where_ref[1]
    me = my_y * WIDE + my_x
    for line, parts in (
        (my_y, (own, own_left, own_right, own_far0, own_far1)),
        (1 - my_y, (other, other_left, other_right, other_far0, other_far1)),
    ):
        for shift, part_ref in ((0, parts[0]), (-1, parts[1]), (1, parts[2])):
            keys_ref[line * WIDE + lax.rem(my_x + shift + WIDE, WIDE)] = part_ref[...]
        far = line * WIDE + lax.rem(my_x + 2, WIDE)
        keys_ref[far, :CUT] = parts[3][...]
        keys_ref[far, CUT:] = parts[4][...]
    queries = qd_ref[...]
    total = total_ref[...]
    acc = acc_ref[...]
    eye = jnp.where(rows_of(HD) == cols_of(HD), 1.0, 0.0).astype(BF16)
    carry = [None] * (SHARDS - 1)
    moved = [None] * (SHARDS - 1)

    def change_of(b):
        return keys_ref[b, LEN : LEN + HD]

    carry[SHARDS - 2] = eye
    for b in range(SHARDS - 3, -1, -1):
        follow = mxu(carry[b + 1], change_of(b + 1), NN)
        carry[b] = jnp.where(b >= me - 1, eye.astype(F32), follow).astype(BF16)
    for b in range(SHARDS - 2, -1, -1):
        moved[b] = mxu(keys_ref[b, :LEN], carry[b], NT).astype(BF16)
        bias = jnp.where(b < me, 0.0, -1e30).astype(F32)
        exped = jnp.exp(mxu(moved[b], queries, NT) + bias)
        total = total + jnp.sum(exped, axis=0, keepdims=True)
        exped = exped.astype(BF16)
        exp_ref[b] = exped
        acc = acc + mxu(keys_ref[b, LEN + HD :], exped, TN)
    inverse_total = 1.0 / total
    core_t = core_ref[...].astype(F32).T
    delta = jnp.sum(core_t * acc, axis=0, keepdims=True) * inverse_total * inverse_total
    delta_ref[...] = delta
    core_t = core_t * inverse_total
    core_scaled = core_t.T.astype(BF16)
    core_scaled_ref[...] = core_scaled
    grad_q = jnp.zeros((HD, LEN), F32)
    inner = jnp.zeros((HD, HD), F32)
    out_ref[SHARDS - 1] = jnp.zeros(out_ref.shape[1:], BF16)
    flow.send(out_ref.at[SHARDS - 1], out_hbm.at[SHARDS - 1])
    flow.send(core_scaled_ref, core_scaled_hbm)
    flow.send(delta_ref, delta_hbm)
    for b in range(SHARDS - 1):
        keys = keys_ref[b, :LEN]
        exped = exp_ref[b]
        change = mxu(keys_ref[b, LEN + HD :], core_scaled, NT)
        grad_scores = (exped.astype(F32) * (change - delta)).astype(BF16)
        grad_q = grad_q + mxu(moved[b], grad_scores, TN)
        through = mxu(grad_scores, queries, NN).astype(BF16)
        out_ref[b, :LEN, :HD] = mxu(through, carry[b], NN).astype(BF16)
        out_ref[b, :LEN, HD:] = mxu(exped, core_scaled, NN).astype(BF16)
        if b >= 1:
            live = jnp.where(b < me, 1.0, 0.0).astype(F32)
            out_map = (one(carry[b], inner, TN) * live).astype(BF16)
        else:
            out_map = jnp.zeros((HD, HD), BF16)
        out_ref[b, LEN:, :HD] = out_map[: HD // 2]
        out_ref[b, LEN:, HD:] = out_map[HD // 2 :]
        flow.send(out_ref.at[b], out_hbm.at[b])
        if b < SHARDS - 2:
            step = mxu(through, keys, TN)
            inner = step if b == 0 else one(inner, change_of(b), NT) + step
    grad_q_ref[...] = TEMP * grad_q
    flow.send(grad_q_ref, grad_q_hbm)
    flow.finish()


def fourth_kernel(
    proj_ref, unit_ref, inv_ref, lrow_ref, y_ref, ut_ref, exp_ref, query_on_ref, query_low_ref,
    key_on_ref, key_low_ref, core_scaled_ref, delta_ref, grad_q_ref,
    dq_ref, dk_ref, dw_ref, gv_ref, taq_ref, vb_ref, low_ref, xtn_ref, fac_ref, fac_low_ref, scale_ref,
):
    queries = unit_ref[:, :HD].astype(BF16)
    keys = unit_ref[:, HD : 2 * HD].astype(BF16)
    reflect_s = split(unit_ref[:, 2 * HD :])
    reflect = reflect_s[0]
    beta_row = 2.0 * jax.nn.sigmoid(lrow_ref[...])
    row, col = rows_of(LEN), cols_of(LEN)
    core_scaled = core_scaled_ref[...]
    exped = exp_ref[...]
    gv_ref[...] = mxu(exped, core_scaled, NN)
    change = one(proj_ref[:, 2 * HD : 3 * HD], core_scaled, NT)
    grad_scores = (TEMP * exped.astype(F32) * (change - delta_ref[...])).astype(BF16)
    grad_q_t = grad_q_ref[...].astype(BF16)
    grad_q = grad_q_t.astype(F32).T.astype(BF16)
    query_on_t = query_on_ref[...]
    key_on_t = (key_on_ref[...], key_low_ref[...])
    inner = mxu(query_on_t, grad_scores, NT) + mxu(query_low_ref[...], grad_scores, NT)
    inner = split(jnp.where(row > col, inner, 0.0))
    side_q = mxu(query_on_t, grad_q, NN) + mxu(query_low_ref[...], grad_q, NN)
    inverse = inv_ref[...]
    factor = split(inverse * beta_row)
    fac_ref[...] = factor[0]
    fac_low_ref[...] = factor[1]
    inverse_t = split(inverse.T)
    taq_ref[...] = three(inverse_t, split(side_q))
    vb_ref[...] = three(inverse_t, reflect_s)
    mid = lower_times_upper_t(inner, key_on_t, three)
    mid = upper_times_lower(inverse_t, split(mid), three)
    low_ref[...] = lower_times_upper_t(split(mid), factor, three)
    diagonal = jnp.sum(jnp.where(row == col, mid, 0.0), axis=1, keepdims=True)
    xtn_ref[...] = upper_times_lower(inverse_t[0], inner[0], mxu).astype(BF16)
    d_query_on = mxu(ut_ref[...], grad_scores, TN) + one(y_ref[...], grad_q, NT)
    d_query_on = -jnp.where(row <= col, d_query_on, 0.0)
    d_query_on = d_query_on.astype(BF16)
    dq_t = grad_q_t.astype(F32) + mxu(keys, grad_scores, TN) + mxu(reflect, d_query_on, TN)
    scales = [unit_scale(proj_ref[:, k * HD : (k + 1) * HD]) for k in (0, 1, 3)]
    dq_ref[...] = unit_back(dq_t.T, unit_ref[:, :HD], scales[0]).astype(BF16)
    lane = lax.broadcasted_iota(jnp.int32, (LEN, HD), 1)
    scale_ref[...] = jnp.where(
        lane < HD // 4, scales[1], jnp.where(lane < HD // 2, scales[2], diagonal)
    )
    dw_ref[...] = mxu(d_query_on, queries, NN)
    dk_ref[...] = mxu(grad_scores, queries, NN)


def unit_back(grad, unit, scale):
    return (grad - unit * jnp.sum(unit * grad, axis=1, keepdims=True)) * scale


def fifth_kernel(
    unit_ref, fac_ref, fac_low_ref, lcol_ref, lrow_ref, y_ref, vt_ref, key_on_ref, key_low_ref,
    dq_ref, dk_ref, dw_ref, gv_ref, taq_ref, vb_ref, low_ref, xtn_ref, scale_ref, back_ref,
    grad_ref,
):
    received = back_ref[0].astype(F32)
    for a in range(1, SHARDS):
        received = received + back_ref[a].astype(F32)
    d_keys = received[:LEN, :HD].astype(BF16)
    d_map = split(jnp.concatenate([received[LEN:, :HD], received[LEN:, HD:]], 0))
    on_keys = mxu(key_on_ref[...], d_keys, NN) + mxu(key_low_ref[...], d_keys, NN)
    side_k = three((fac_ref[...], fac_low_ref[...]), split(on_keys))
    vb = vb_ref[...]
    vb_s = split(vb)
    side_q = taq_ref[...] + three(vb_s, d_map)
    beta_col = 2.0 * jax.nn.sigmoid(lcol_ref[...])
    beta_row = 2.0 * jax.nn.sigmoid(lrow_ref[...])
    row, col = rows_of(LEN), cols_of(LEN)
    y_s = split(y_ref[...])
    d_system = low_ref[...] + three(split(side_q), y_s, NT) + three(vb_s, split(side_k), NT)
    d_system = jnp.where(row > col, d_system, 0.0)
    dw = dw_ref[...] - side_k - three(y_s, d_map, NT) - beta_col * side_q
    keys = unit_ref[:, HD : 2 * HD]
    reflect = unit_ref[:, 2 * HD :]
    reflect_s = split(reflect)
    diagonal = scale_ref[:, HD - 1 :] + jnp.sum(
        side_q * reflect + vb * on_keys, axis=1, keepdims=True
    )
    gram = three(reflect_s, reflect_s, NT)
    d_beta = split(jnp.where(row == col, -diagonal, 0.0) + d_system * gram)
    ones = jnp.ones((TALL - LEN, LEN), BF16)
    d_beta = mxu(ones, d_beta[0], NT) + mxu(ones, d_beta[1], NT)
    d_logit = d_beta * beta_row * (1.0 - 0.5 * beta_row)
    first = lax.broadcasted_iota(jnp.int32, (TALL - LEN, LEN), 0) == 0
    grad_ref[LEN:] = jnp.where(first, d_logit, 0.0).astype(BF16)
    d_gram = split(beta_col * d_system)
    dw = dw + three(d_gram, reflect_s, NN)
    dw_t = three(reflect_s, d_gram, TN)
    d_key_on = beta_col * xtn_ref[...].astype(F32) + one(vt_ref[...], d_keys.T, TN)
    d_key_on = -jnp.where(row > col, d_key_on, 0.0)
    d_key_on = d_key_on.astype(BF16)
    dk_t = mxu(reflect_s[0], d_key_on, TN)
    dw = dw + one(d_key_on, keys, NN) + dw_t.T
    dk = d_keys.astype(F32) + dk_ref[...] + dk_t.T
    grad_ref[:LEN, 2 * HD : 3 * HD] = (gv_ref[...] + received[:LEN, HD:]).astype(BF16)
    grad_ref[:LEN, :HD] = dq_ref[...]
    grad_ref[:LEN, HD : 2 * HD] = unit_back(dk, keys, scale_ref[:, :1]).astype(BF16)
    side = scale_ref[:, HD // 4 : HD // 4 + 1]
    grad_ref[:LEN, 3 * HD :] = unit_back(dw, reflect, side).astype(BF16)


def shape(*dims, dtype=F32):
    return jax.ShapeDtypeStruct(dims, dtype)


class Flow:
    def __init__(self, semaphores):
        self.semaphores = semaphores
        self.used = 0
        self.open = []

    def fetch(self, source, target):
        copy = pltpu.make_async_copy(source, target, self.semaphores.at[self.used])
        self.used += 1
        copy.start()
        return copy

    def send(self, source, target):
        self.open.append(self.fetch(source, target))

    def finish(self):
        for copy in self.open:
            copy.wait()


VMEM = pl.BlockSpec(memory_space=pltpu.VMEM)
SMEM = pl.BlockSpec(memory_space=pltpu.SMEM)
HBM = pl.BlockSpec(memory_space=pltpu.HBM)


class Late:
    def __init__(self, ref, copy):
        self.ref = ref
        self.copy = copy

    def __getitem__(self, index):
        if self.copy is not None:
            self.copy.wait()
            self.copy = None
        return self.ref[index]


class Early:
    def __init__(self, flow, ref, target):
        self.flow = flow
        self.ref = ref
        self.target = target

    def __setitem__(self, index, value):
        self.ref[index] = value
        self.flow.send(self.ref, self.target)


def build(kernel, outs, args, in_specs, out_specs, scratch, copies, limit=32):
    def body(*refs):
        kernel(Flow(refs[-1]), *refs[:-1])

    single = not isinstance(outs, list)
    if single:
        outs, out_specs = [outs], [out_specs]
    args = [
        pltpu.with_memory_space_constraint(arg, pltpu.HBM) if spec is HBM else arg
        for arg, spec in zip(args, in_specs)
    ]
    outs = [
        pltpu.HBM(out.shape, out.dtype) if spec is HBM else out
        for out, spec in zip(outs, out_specs)
    ]
    results = pl.pallas_call(
        body,
        out_shape=outs,
        in_specs=in_specs,
        out_specs=out_specs,
        scratch_shapes=list(scratch) + [pltpu.SemaphoreType.DMA((copies,))],
        compiler_params=pltpu.CompilerParams(vmem_limit_bytes=limit * 2**20),
        cost_estimate=pl.CostEstimate(
            flops=2 * 10**9, bytes_accessed=4 * 2**20, transcendentals=0
        ),
    )(*args)
    return results[0] if single else results


def call(kernel, outs, *args, far_in=(), far_out=(), limit=32):
    far_in, far_out = tuple(far_in), tuple(far_out)
    count = len(args)

    def body(flow, *refs):
        ins, results = list(refs[:count]), list(refs[count : count + len(outs)])
        buffers = list(refs[count + len(outs) :])
        for i in far_in:
            buffer = buffers.pop(0)
            ins[i] = Late(buffer, flow.fetch(ins[i], buffer))
        for i in far_out:
            results[i] = Early(flow, buffers.pop(0), results[i])
        kernel(*ins, *results)
        flow.finish()

    return build(
        body,
        outs,
        args,
        [HBM if i in far_in else VMEM for i in range(count)],
        [HBM if i in far_out else VMEM for i in range(len(outs))],
        [pltpu.VMEM(args[i].shape, args[i].dtype) for i in far_in]
        + [pltpu.VMEM(outs[i].shape, outs[i].dtype) for i in far_out],
        max(1, len(far_in) + len(far_out)),
        limit,
    )


def project_kernel(offsets):
    def body(flow, where_ref, bias_ref, own_ref, swap_ref, weight_hbm, beta_ref, *refs):
        later = len(refs) == 9
        before = refs[:3] if later else None
        all_hbm, proj_ref, col_ref, row_ref, all_ref, weight_ref = refs[-6:]
        my_z, my_y, my_core = where_ref[2], where_ref[3], where_ref[4]
        places = [lax.rem(my_z + offset + DEPTH, DEPTH) for offset in offsets]
        copies = [
            flow.fetch(weight_hbm.at[pl.ds(pl.multiple_of(z * LEN, LEN), LEN)], weight_ref.at[k])
            for k, z in enumerate(places)
        ]
        for k in range(len(offsets)):
            for side in range(2):
                base = 2 * (my_y if side == 0 else 1 - my_y)
                all_ref[k, base + my_core] = own_ref[k, side]
                all_ref[k, base + 1 - my_core] = swap_ref[k, side]
            flow.send(all_ref.at[k], all_hbm.at[k])
        proj = before[0][...] if later else jnp.zeros((LEN, 4 * HD), F32)
        col = before[1][...] if later else jnp.zeros((LEN, 8), F32) + bias_ref[0]
        row = before[2][...] if later else jnp.zeros((8, LEN), F32) + bias_ref[0]
        for k, z in enumerate(places):
            features = jnp.concatenate([all_ref[k, j] for j in range(4)], axis=1)
            beta = jnp.broadcast_to(beta_ref[z], (8, LEN)).astype(BF16)
            col = col + mxu(features, beta, NT)
            row = row + mxu(beta, features, NT)
            copies[k].wait()
            proj = proj + mxu(features, weight_ref[k], NN)
        proj_ref[...] = proj
        col_ref[...] = col
        row_ref[...] = row
        flow.finish()

    return body


def project(offsets, where, bias, own, swap, weights, betas, before=()):
    count = len(offsets)
    return build(
        project_kernel(offsets),
        [
            shape(count, 4, LEN, HD, dtype=BF16),
            shape(LEN, 4 * HD),
            shape(LEN, 8),
            shape(8, LEN),
        ],
        (where, bias, own, swap, weights, betas) + tuple(before),
        [SMEM, SMEM, VMEM, VMEM, HBM, VMEM] + [VMEM] * len(before),
        [HBM, VMEM, VMEM, VMEM],
        [
            pltpu.VMEM((count, 4, LEN, HD), BF16),
            pltpu.VMEM((count, LEN, 4 * HD), BF16),
        ],
        2 * count,
    )


def weight_kernel(flow, where_ref, near_hbm, far_hbm, grad_ref, out_hbm, flip_hbm, all_ref, out_ref, flip_ref):
    my_z = where_ref[2]
    copies = [
        flow.fetch(near_hbm.at[k] if k < 5 else far_hbm.at[k - 5], all_ref.at[k])
        for k in range(DEPTH)
    ]
    for k, offset in enumerate(OFFSETS):
        copies[k].wait()
        z = lax.rem(my_z + offset + DEPTH, DEPTH)
        flipped = jnp.concatenate([all_ref[k, j].T for j in range(4)], axis=0)
        flip_ref[k] = flipped
        flow.send(flip_ref.at[k], flip_hbm.at[z])
        out_ref[k] = mxu(flipped, grad_ref[...], NN).astype(BF16)
        flow.send(out_ref.at[k], out_hbm.at[z])
    flow.finish()


def rest_kernel(flow, flip_hbm, grad_ref, out_hbm, flip_ref, out_ref):
    copies = [flow.fetch(flip_hbm.at[k], flip_ref.at[k]) for k in range(SHARDS)]
    grad = grad_ref[:LEN, HD:]
    logit = grad_ref[LEN:]
    rest = jnp.zeros((TALL - LEN, 2 * HD), BF16)
    for k in range(SHARDS):
        copies[k].wait()
        flipped = flip_ref[k]
        out_ref[k, :LEN] = mxu(flipped, grad, NN).astype(BF16)
        beta = mxu(logit, flipped, NT).astype(BF16)
        out_ref[k, LEN:TALL] = beta[:, : LEN - HD]
        out_ref[k, TALL:] = jnp.concatenate([beta[:, LEN - HD :], rest], axis=1)
        flow.send(out_ref.at[k], out_hbm.at[k])
    flow.finish()


def query_sums(where, near_all, far_all, grad):
    outs = [shape(SHARDS, LEN, HD, dtype=BF16), shape(SHARDS, LEN, LEN, dtype=BF16)]
    return build(
        weight_kernel,
        outs,
        (where, near_all, far_all, grad),
        [SMEM, HBM, HBM, VMEM],
        [HBM, HBM],
        [pltpu.VMEM((DEPTH, 4, LEN, HD), BF16)] + [pltpu.VMEM(o.shape, o.dtype) for o in outs],
        3 * DEPTH,
    )


def rest_sums(flipped, grad):
    out = shape(SHARDS, TALL + TALL - LEN, 3 * HD, dtype=BF16)
    return build(
        rest_kernel,
        out,
        (flipped, grad),
        [HBM, VMEM],
        HBM,
        [pltpu.VMEM(flipped.shape, BF16), pltpu.VMEM(out.shape, BF16)],
        2 * SHARDS,
    )


def total_kernel(queries_ref, rest_ref, weight_ref, beta_ref):
    for ref, columns in ((queries_ref, slice(0, HD)), (rest_ref, slice(HD, 4 * HD))):
        total = ref[0, :LEN].astype(F32)
        for a in range(1, SHARDS):
            total = total + ref[a, :LEN].astype(F32)
        weight_ref[:, columns] = total.astype(BF16)
    beta = rest_ref[0, LEN:].astype(F32)
    for a in range(1, SHARDS):
        beta = beta + rest_ref[a, LEN:].astype(F32)
    extra = TALL - LEN
    beta_ref[...] = jnp.concatenate([beta[:1], beta[extra : extra + 1, :HD]], axis=1)


def feature_kernel(offsets):
    def body(
        flow, where_ref, own_ref, other_ref, weight_hbm, away_hbm, own_beta, other_beta, out_ref,
        weight_ref, away_ref,
    ):
        my_z, my_y, my_core = where_ref[2], where_ref[3], where_ref[4]
        extra = TALL - LEN
        places = [lax.rem(my_z + offset + DEPTH, DEPTH) for offset in offsets]
        copies = []
        for k, z in enumerate(places):
            base = pl.multiple_of(z * LEN + my_core * HD, HD)
            copies.append(
                [
                    flow.fetch(weight_hbm.at[pl.ds(base, HD)], weight_ref.at[k, :HD]),
                    flow.fetch(weight_hbm.at[pl.ds(base + HALF, HD)], weight_ref.at[k, HD:]),
                    flow.fetch(away_hbm.at[z], away_ref.at[k]),
                ]
            )
        own, other = own_ref[:LEN], other_ref[:LEN]
        logits = jnp.concatenate([own_ref[LEN:], other_ref[LEN:]], axis=0)
        for k, z in enumerate(places):
            betas = jnp.concatenate(
                [
                    jnp.broadcast_to(own_beta[z], (extra, HALF)),
                    jnp.broadcast_to(other_beta[z], (extra, HALF)),
                ],
                axis=0,
            ).astype(BF16)
            for copy in copies[k]:
                copy.wait()
            term = mxu(own, weight_ref[k], NT) + mxu(other, away_ref[k], NT)
            term = (term + mxu(logits, betas, TN)).astype(BF16)
            out_ref[k, my_y] = term[:, :HD]
            out_ref[k, 1 - my_y] = term[:, HD:]

    return body


def features(offsets, *args):
    count = len(offsets)
    return build(
        feature_kernel(offsets),
        shape(count, 2, LEN, HD, dtype=BF16),
        args,
        [SMEM, VMEM, VMEM, HBM, HBM, VMEM, VMEM],
        VMEM,
        [pltpu.VMEM((count, HALF, 4 * HD), BF16), pltpu.VMEM((count, HALF, 4 * HD), BF16)],
        3 * count,
    )


def swapped(value, axis):
    return lax.ppermute(value, axis, [(0, 1), (1, 0)])


def turned(value, axis, step):
    count = lax.axis_size(axis)
    return lax.ppermute(value, axis, [(i, (i + step) % count) for i in range(count)])


def plus(*terms):
    total = terms[0].astype(F32)
    for term in terms[1:]:
        total = total + term.astype(F32)
    return total


def line_of(block):
    left, right = turned(block, "x", 1), turned(block, "x", -1)
    return block, left, right, turned(left[:CUT], "x", 1), turned(right[CUT:], "x", -1)


def scatter_heads(at, beside):
    up = turned(at(-4)[0], "z", 1)
    down = turned(at(-4)[1], "z", -1)
    up = jnp.stack([plus(at(3)[0], up).astype(BF16), at(3)[1]])
    down = jnp.stack([at(-3)[0], plus(at(-3)[1], down).astype(BF16)])
    for step in (2, 1):
        up = plus(turned(up, "z", 1), at(step)).astype(BF16)
        down = plus(turned(down, "z", -1), at(-step)).astype(BF16)
    total = plus(turned(up, "z", 1), turned(down, "z", -1), at(0))
    received, beside = lax.optimization_barrier(
        (swapped(total[1].astype(BF16), "y_hi"), beside)
    )
    return total[0] + received.astype(F32), beside


def on_device(layer_input, grad_core, w_in, beta_proj, beta_bias):
    where = jnp.stack([lax.axis_index(axis) for axis in CTX + HEAD]).astype(jnp.int32)
    core = lax.axis_index("core")
    betas = beta_proj[0].astype(F32).reshape(DEPTH, 1, LEN)
    beta_by_core = beta_proj[0].reshape(2 * DEPTH, 2, HD)
    own_beta = lax.dynamic_index_in_dim(beta_by_core, core, 1, False).reshape(DEPTH, 1, HALF)
    away_beta = lax.dynamic_index_in_dim(beta_by_core, 1 - core, 1, False)
    away_beta = swapped(away_beta.reshape(DEPTH, 1, HALF), "core").astype(F32)
    own_beta = own_beta.astype(F32)
    pair = jnp.stack([layer_input, swapped(layer_input, "y_hi")])
    up, down = turned(pair, "z", 1), turned(pair, "z", -1)
    weights = w_in.reshape(w_in.shape[0], 4 * HD)
    up, down, weights, where, betas, own_beta = lax.optimization_barrier(
        (up, down, weights, where, betas, own_beta)
    )
    up_two, down_two = turned(up, "z", 1), turned(down, "z", -1)
    by_core = weights.reshape(2 * DEPTH, 2, HD, 4 * HD)
    away = lax.dynamic_index_in_dim(by_core, 1 - core, 1, False).reshape(DEPTH, HALF, 4 * HD)
    up_two, down_two, away, away_beta = lax.optimization_barrier(
        (up_two, down_two, away, away_beta)
    )
    near = jnp.stack([pair, up, down, up_two, down_two])
    near_swap = swapped(near, "core")
    up_three, down_three = turned(up_two, "z", 1), turned(down_two, "z", -1)
    last = jnp.stack([turned(up_three[0], "z", 1), turned(down_three[1], "z", -1)])
    near_all, *partial = project(NEAR, where, beta_bias, near, near_swap, weights, betas)
    far = jnp.stack([up_three, down_three, last])
    far_swap = swapped(far, "core")
    far_all, projected, logit_col, logit_row = project(
        FAR, where, beta_bias, far, far_swap, weights, betas, partial
    )
    logit_col, logit_row = logit_col[:, :1], logit_row[:1]
    sent, inverse, unit, y_side, vt_side, *twins = call(
        first_kernel,
        [
            shape(PACK, HD, dtype=BF16),
            shape(LEN, LEN),
            shape(LEN, 3 * HD),
            shape(LEN, HD),
            shape(HD, LEN),
            shape(LEN, LEN),
            shape(LEN, 3 * HD),
            shape(LEN, HD),
        ],
        projected,
        logit_col,
        logit_row,
        far_out=(1, 2, 3, 4),
    )
    square = shape(LEN, LEN, dtype=BF16)
    query_dev, ut_side, exp_in, query_on, query_low, key_on, key_low, total_in, acc_in = call(
        second_kernel,
        [shape(LEN, HD, dtype=BF16)] + [square] * 6 + [shape(1, LEN), shape(HD, LEN)],
        twins[1],
        twins[0],
        logit_row,
        twins[2],
        sent,
        far_out=(1, 2, 3, 4, 5, 6),
    )
    other, query_dev = lax.optimization_barrier((swapped(sent, "y_lo"), query_dev))
    shards = line_of(sent) + line_of(other)
    back, grad_query, core_scaled, delta = build(
        third_kernel,
        [
            shape(SHARDS, LEN + HD // 2, 2 * HD, dtype=BF16),
            shape(HD, LEN),
            shape(LEN, HD, dtype=BF16),
            shape(1, LEN),
        ],
        (where, query_dev, *shards, grad_core, total_in, acc_in),
        [SMEM] + [VMEM] * 14,
        [HBM] * 4,
        [
            pltpu.VMEM((SHARDS - 1, LEN, LEN), BF16),
            pltpu.VMEM((SHARDS, PACK, HD), BF16),
            pltpu.VMEM((SHARDS, LEN + HD // 2, 2 * HD), BF16),
            pltpu.VMEM((HD, LEN), F32),
            pltpu.VMEM((LEN, HD), BF16),
            pltpu.VMEM((1, LEN), F32),
        ],
        SHARDS + 3,
    )
    returned = lax.all_to_all(back, CTX, 0, 0)
    away = swapped(away, "core")
    column = shape(LEN, HD)
    outs = call(
        fourth_kernel,
        [shape(LEN, HD, dtype=BF16)]
        + [column] * 5
        + [shape(LEN, LEN)]
        + [square] * 3
        + [column],
        projected,
        unit,
        inverse,
        logit_row,
        y_side,
        ut_side,
        exp_in,
        query_on,
        query_low,
        key_on,
        key_low,
        core_scaled,
        delta,
        grad_query,
        far_in=(0, 1, 2, 4, 5, 6, 7, 8, 9, 10, 11, 13),
        far_out=range(11),
    )
    dq, dk, dw, gv, taq, vb, low, xtn, factor, factor_low, scale = outs
    queries_w, flipped = query_sums(where, near_all, far_all, dq)
    returned, queries_w = lax.optimization_barrier((returned, queries_w))
    queries_w = lax.all_to_all(queries_w, CTX, 0, 0)
    grad_proj = call(
        fifth_kernel,
        [shape(TALL, 4 * HD, dtype=BF16)],
        unit,
        factor,
        factor_low,
        logit_col,
        logit_row,
        y_side,
        vt_side,
        key_on,
        key_low,
        dq,
        dk,
        dw,
        gv,
        taq,
        vb,
        low,
        xtn,
        scale,
        returned,
        far_in=(7, 8, 1, 2, 13, 14, 5, 15, 11, 0, 16, 6, 10, 17, 12, 9),
    )[0]
    other_proj = swapped(grad_proj, "core")
    sides = (where, grad_proj, other_proj, weights, away, own_beta, away_beta)
    first, second = (-4, 3, -3, 2, -2), (1, -1, 0)
    first_terms = features(first, *sides)
    second_terms = features(second, *sides)

    def at(offset):
        if offset in first:
            return first_terms[first.index(offset)]
        return second_terms[second.index(offset)]

    rest_w = rest_sums(flipped, grad_proj)
    rest_w = lax.all_to_all(rest_w, CTX, 0, 0)
    grad_w_in, grad_beta = call(
        total_kernel,
        [shape(LEN, 4 * HD, dtype=BF16), shape(1, 4 * HD)],
        queries_w,
        rest_w,
        far_in=(0, 1),
    )
    grad_input, (grad_w_in, grad_beta) = scatter_heads(
        at, (grad_w_in.reshape(LEN, 1, 4, HD), grad_beta)
    )
    return (grad_input.astype(BF16), grad_w_in, grad_beta)


def solution(mesh):
    parts = Mesh(mesh.devices.reshape(2, WIDE, DEPTH, 2, 2), CTX + HEAD)
    in_specs = (P(CTX, HEAD), P(CTX, HEAD), P(None, HEAD, None, None), P(HEAD, None), P(HEAD))
    out_specs = (P(CTX, HEAD), P(CTX, HEAD, None, None), P(HEAD, CTX))
    return jax.shard_map(
        on_device, mesh=parts, in_specs=in_specs, out_specs=out_specs, check_vma=False
    )
```
